32 devices in a mesh: row: 4 (over z), col: 8 (over y, x, core).
Axes of the slice: x: 2, y: 2, z: 4, core: 2. Of those that a mesh axis runs over, the one named last changes fastest.
Arguments:
- ancestor_inverse: float32 [16384, 16384], P('row', 'col'), may hold values from -6 to 6
- panel_one: bfloat16 [16384, 256], P(('row', 'col')), may hold values from -0.046875 to 0.046875
- panel_two: bfloat16 [16384, 256], P(('row', 'col')), may hold values from -0.046875 to 0.046875
- panel_three: bfloat16 [16384, 256], P(('row', 'col')), may hold values from -0.046875 to 0.046875
- couplings: bfloat16 [3, 256, 256], replicated, may hold values from -0.375 to 0.375
- diag_terms: float32 [3, 256, 256], replicated, may hold values from -6 to 6
- list_two: int32 [60], replicated, may hold values from 0 to 63, as said below
- list_three: int32 [56], replicated, may hold values from 0 to 63, as said below
Outputs:
- inverse_one: float32 [16384, 256], P(('row', 'col'))
- inverse_two: float32 [16384, 256], P(('row', 'col'))
- inverse_three: float32 [16384, 256], P(('row', 'col'))
- small_blocks: float32 [6, 256, 256], P(None, 'row', 'col')
The draws below stay inside these ranges and needn't reach their ends.
Inputs may be any that keep to these rules, and one draw needn't show every extreme that they name: `list_two`: 60 distinct block indices in increasing order, always including 0 and 63. `list_three`: 56 distinct entries of list_two in increasing order, always including 0 and 63.
All inputs are finite; a program needn't handle non-finite values.
Results may differ from the reference program's by a relative error of at most 0.0003.
Values may be sent and summed in bfloat16 or wider, within the bound.
No kernel may reach another device: no remote copies, remote signals or barrier semaphores. Data moves between devices by JAX's collectives and lax.ppermute only.
A program may use at most 128 MiB of HBM per device.

```python
import jax
import jax.numpy as jnp
from jax import lax

W = 256
NB = 64
B2 = 60
B3 = 56
R = 16384


def pick_lists(key):
    inner_ids = 1 + jax.random.permutation(jax.random.fold_in(key, 7101), NB - 2).astype(jnp.int32)
    chosen = inner_ids[:B2 - 2]
    first_block = jnp.zeros((1,), jnp.int32)
    last_block = jnp.full((1,), NB - 1, jnp.int32)
    listed_two = jnp.sort(jnp.concatenate([first_block, chosen, last_block]))
    shuffled = jax.random.permutation(jax.random.fold_in(key, 7102), B2 - 2).astype(jnp.int32)
    kept_ids = chosen[shuffled[:B3 - 2]]
    listed_three = jnp.sort(jnp.concatenate([first_block, kept_ids, last_block]))
    return (listed_two, listed_three)


def draw_list_two(key, part):
    return pick_lists(key)[0]


def draw_list_three(key, part):
    return pick_lists(key)[1]


def raised(drawn, own_key, source, target, shards_of, factor):
    owner, partner = [(jnp.arange(drawn.shape[dim]) // (drawn.shape[dim] // shards_of)).reshape([-1 if axis == dim else 1 for axis in range(drawn.ndim)]) for dim in (source, target)]
    chosen = jax.random.permutation(own_key, shards_of)[partner]
    strong = (owner == chosen) | (owner == (partner + shards_of // 2) % shards_of)
    return jnp.where(strong, factor * drawn, drawn)


def shard_levels(key, dims, split, smallest, high):
    level, own = 1.0, jax.random.fold_in(key, 6)
    for dim, parts in split:
        draws = jnp.exp(jax.random.uniform(jax.random.fold_in(own, dim), (parts,), jnp.float32, smallest / len(split), high / len(split)))
        level = level * jnp.repeat(draws, dims[dim] // parts).reshape([-1 if axis == dim else 1 for axis in range(len(dims))])
    return level


def centred(stream_key, shape, width, bound, pieces=(), kind=jnp.bfloat16):
    array = width * jax.random.normal(stream_key, shape, jnp.float32)
    if pieces:
        array = array * shard_levels(stream_key, shape, pieces, -0.22, 0.18)
    return jnp.clip(array, -bound, bound).astype(kind)


def gaussian_with(rng, dims, spread, bound, pieces, heavy, kind=jnp.bfloat16):
    entries = spread * jax.random.normal(rng, dims, jnp.float32)
    if pieces:
        entries = entries * shard_levels(rng, dims, pieces, -0.22, 0.18)
    return jnp.clip(raised(entries, jax.random.fold_in(rng, 3), *heavy), -bound, bound).astype(kind)


def setup_inputs(seed: int = 0) -> dict:
    arg_keys = jax.random.split(jax.random.key(seed), 9)
    return {
        "ancestor_inverse": gaussian_with(arg_keys[0], (R, R), 1.0, 6.0, ((0, 4), (1, 8)), (1, 0, 8, 2.0), jnp.float32),
        "panel_one": centred(arg_keys[1], (R, W), (NB * W) ** -0.5, 0.046875, ((0, 32),)),
        "panel_two": centred(arg_keys[2], (R, W), (NB * W) ** -0.5, 0.046875, ((0, 32),)),
        "panel_three": centred(arg_keys[3], (R, W), (NB * W) ** -0.5, 0.046875, ((0, 32),)),
        "couplings": centred(arg_keys[4], (3, W, W), W ** -0.5, 0.375),
        "diag_terms": centred(arg_keys[5], (3, W, W), 1.0, 6.0, (), jnp.float32),
        "list_two": draw_list_two(jax.random.fold_in(arg_keys[8], 71), 0),
        "list_three": draw_list_three(jax.random.fold_in(arg_keys[8], 71), 0),
    }


def product(former, latter):
    return jnp.dot(former, latter, precision=lax.Precision.HIGHEST, preferred_element_type=jnp.float32)


def inner_product(former, latter):
    return lax.dot_general(former, latter, (((0,), (0,)), ((), ())), precision=lax.Precision.HIGHEST, preferred_element_type=jnp.float32)


def row_keep(listed):
    blocks = jnp.arange(NB * W, dtype=jnp.int32) // W
    matches = blocks[:, None] == listed[None, :].astype(jnp.int32)
    return jnp.any(matches, axis=1).astype(jnp.float32)[:, None]


def reference(ancestor_inverse, panel_one, panel_two, panel_three, couplings, diag_terms, list_two, list_three):
    keep_two = row_keep(list_two)
    keep_three = row_keep(list_three)
    factor_one = panel_one.astype(jnp.float32)
    factor_two = panel_two.astype(jnp.float32) * keep_two
    factor_three = panel_three.astype(jnp.float32) * keep_three
    coupled = couplings.astype(jnp.float32)
    inverse_one = -product(ancestor_inverse, factor_one)
    diag_one = diag_terms[0] - inner_product(factor_one, inverse_one)
    inverse_two = -(product(ancestor_inverse, factor_two) + product(inverse_one, coupled[0])) * keep_two
    cross_two = -(inner_product(inverse_one, factor_two) + product(diag_one, coupled[0]))
    diag_two = diag_terms[1] - inner_product(factor_two, inverse_two) - inner_product(coupled[0], cross_two)
    inverse_three = -(product(ancestor_inverse, factor_three) + product(inverse_one, coupled[1]) + product(inverse_two, coupled[2])) * keep_three
    cross_first = -(inner_product(inverse_one, factor_three) + product(diag_one, coupled[1]) + product(cross_two, coupled[2]))
    cross_second = -(inner_product(inverse_two, factor_three) + inner_product(cross_two, coupled[1]) + product(diag_two, coupled[2]))
    diag_three = diag_terms[2] - inner_product(factor_three, inverse_three) - inner_product(coupled[1], cross_first) - inner_product(coupled[2], cross_second)
    stacked = jnp.stack([diag_one, diag_two, diag_three, cross_two, cross_first, cross_second])
    return inverse_one, inverse_two, inverse_three, stacked
```

```python
import functools

import jax
import jax.numpy as jnp
from jax import lax
from jax.experimental import pallas as pl
from jax.experimental.pallas import tpu as pltpu
from jax.sharding import PartitionSpec as P

F32 = jnp.float32
BF16 = jnp.bfloat16


def product(former, latter):
    return jnp.dot(
        former, latter, precision=lax.Precision.HIGHEST, preferred_element_type=F32
    )


def inner_product(former, latter):
    return lax.dot_general(
        former,
        latter,
        (((0,), (0,)), ((), ())),
        precision=lax.Precision.HIGHEST,
        preferred_element_type=F32,
    )


def piece_keep(listed, start_row, slab_rows, block_width):
    rows_here = start_row + jnp.arange(slab_rows, dtype=jnp.int32)
    matches = (rows_here // block_width)[:, None] == listed[None, :]
    return jnp.any(matches, axis=1).astype(F32)[:, None]


def spread_panel(own, rows, cols):
    ratio = cols // rows
    received = []
    for step in range(rows):
        pairs = []
        for plane in range(rows):
            for place in range(cols):
                target = ((place % rows) ^ step) * cols + plane * ratio + place // rows
                pairs.append((plane * cols + place, target))
        received.append(lax.ppermute(own, ("row", "col"), pairs))
    return received


def multiply_kernel(where, s_ref, *refs):
    pieces, out_ref, panel = refs[:-2], refs[-2], refs[-1]
    depth = pieces[0].shape[0]

    @pl.when((pl.program_id(0) == 0) & (pl.program_id(1) == 0))
    def _():
        for step, piece in enumerate(pieces):
            begin = pl.multiple_of((where[0] ^ step) * depth, depth)
            panel[pl.ds(begin, depth), :] = piece[...]

    whole = s_ref[...]
    high = whole.astype(BF16)
    low = (whole - high.astype(F32)).astype(BF16)
    factor = panel[...]
    out_ref[0] = jnp.dot(high, factor, preferred_element_type=F32) + jnp.dot(
        low, factor, preferred_element_type=F32
    )


def multiply(where, ancestor, pieces, slab_rows):
    local_rows, local_cols = ancestor.shape
    width = pieces[0].shape[1]
    chips = local_rows // slab_rows // 2
    tile = min(256, slab_rows)
    tiles = slab_rows // tile
    grid_spec = pltpu.PrefetchScalarGridSpec(
        num_scalar_prefetch=1,
        grid=(chips, tiles),
        in_specs=[
            pl.BlockSpec(
                (tile, local_cols), lambda i, j, where: ((2 * i + where[1]) * tiles + j, 0)
            )
        ]
        + [pl.BlockSpec(piece.shape, lambda i, j, where: (0, 0)) for piece in pieces],
        out_specs=pl.BlockSpec((1, tile, width), lambda i, j, where: (i, j, 0)),
        scratch_shapes=[pltpu.VMEM((local_cols, width), BF16)],
    )
    flops = 2 * 2 * chips * slab_rows * local_cols * width
    return pl.pallas_call(
        multiply_kernel,
        grid_spec=grid_spec,
        out_shape=jax.ShapeDtypeStruct((chips, slab_rows, width), F32),
        compiler_params=pltpu.CompilerParams(vmem_limit_bytes=28 * 1024 * 1024),
        cost_estimate=pl.CostEstimate(
            flops=flops,
            bytes_accessed=4 * chips * slab_rows * (local_cols + width),
            transcendentals=0,
        ),
    )(where, ancestor, *pieces)


def sibling(value, cols):
    return lax.ppermute(value, "col", [(c, c ^ 1) for c in range(cols)])


def to_chip(value, step, cols):
    return lax.ppermute(value, "col", [(c, c ^ (2 * step)) for c in range(cols)])


def take(pieces, index):
    return lax.dynamic_index_in_dim(pieces, index, 0, keepdims=False)


def chip_scatter(summed, cols):
    chip = lax.axis_index("col") // 2
    total = take(summed, chip)
    arrived = [to_chip(take(summed, chip ^ step), step, cols) for step in range(1, cols // 2)]
    for piece in arrived:
        total = total + piece
    return total


def panel_sum(where, other_where, ancestor, pieces, slab_rows, cols):
    theirs = multiply(other_where, ancestor, pieces, slab_rows)
    handed = sibling(theirs, cols)
    mine = multiply(where, ancestor, pieces, slab_rows)
    return chip_scatter(mine + handed, cols)


def tile_scatter(blocks, rows, cols):
    count, width = blocks.shape[0], blocks.shape[1]
    part = width // cols
    core = lax.axis_index("col") % 2
    split = blocks.reshape(count, cols // 2, 2, part, width)
    split = jnp.moveaxis(split, 0, 2)
    split = jnp.moveaxis(split, 1, 0)
    mine = take(split, core)
    handed = sibling(take(split, 1 - core), cols)
    strip = chip_scatter(mine + handed, cols)
    row = lax.axis_index("row")
    high = width // rows

    def rows_of(index):
        return lax.dynamic_slice_in_dim(strip, index * high, high, 2)

    total = rows_of(row)
    for step in range(1, rows):
        pairs = [(r, r ^ step) for r in range(rows)]
        total = total + lax.ppermute(rows_of(row ^ step), "row", pairs)
    return jnp.swapaxes(total, 1, 2)


def body(
    rows,
    cols,
    ancestor,
    panel_one,
    panel_two,
    panel_three,
    couplings,
    diag_terms,
    list_two,
    list_three,
):
    block_width = couplings.shape[1]
    slab_rows = panel_one.shape[0]
    row_id, col_id = lax.axis_index("row"), lax.axis_index("col")
    device = row_id * cols + col_id
    where = jnp.stack([row_id, col_id % 2]).astype(jnp.int32)
    other_where = jnp.stack([row_id, 1 - col_id % 2]).astype(jnp.int32)
    spread_one = spread_panel(panel_one, rows, cols)
    keep_two = piece_keep(list_two, device * slab_rows, slab_rows, block_width)
    keep_three = piece_keep(list_three, device * slab_rows, slab_rows, block_width)
    own_two = jnp.where(keep_two > 0.5, panel_two, jnp.zeros_like(panel_two))
    own_three = jnp.where(keep_three > 0.5, panel_three, jnp.zeros_like(panel_three))
    spread_two = spread_panel(own_two, rows, cols)
    spread_three = spread_panel(own_three, rows, cols)
    coupled = couplings.astype(F32)
    ends = jnp.where(device == 0, diag_terms, jnp.zeros_like(diag_terms))
    factors = [panel_one.astype(F32), own_two.astype(F32), own_three.astype(F32)]

    scatter = functools.partial(
        panel_sum, where, other_where, ancestor, slab_rows=slab_rows, cols=cols
    )
    sum_one = scatter(spread_one)
    m_oneone = inner_product(factors[0], sum_one)
    m_twoone = inner_product(factors[1], sum_one)
    m_threeone = inner_product(factors[2], sum_one)
    inverse_one = -sum_one

    sum_two = scatter(spread_two)
    m_twotwo = inner_product(factors[1], sum_two)
    m_threetwo = inner_product(factors[2], sum_two)
    inverse_two = -(sum_two - product(sum_one, coupled[0])) * keep_two

    diag_one = ends[0] + m_oneone
    cross_two = m_twoone.T - product(diag_one, coupled[0])
    diag_two = (
        ends[1] + m_twotwo - product(m_twoone, coupled[0]) - inner_product(coupled[0], cross_two)
    )
    second_three = m_threetwo - product(m_threeone, coupled[0])
    cross_first = m_threeone.T - product(diag_one, coupled[1]) - product(cross_two, coupled[2])
    cross_second = (
        second_three.T - inner_product(cross_two, coupled[1]) - product(diag_two, coupled[2])
    )
    most_three = (
        ends[2]
        - product(m_threeone, coupled[1])
        - product(second_three, coupled[2])
        - inner_product(coupled[1], cross_first)
        - inner_product(coupled[2], cross_second)
    )
    early = jnp.stack(
        [diag_one.T, diag_two.T, most_three.T, cross_two.T, cross_first.T, cross_second.T]
    )
    early_tile = tile_scatter(early, rows, cols)

    sum_three = scatter(spread_three)
    m_threethree = inner_product(sum_three, factors[2])
    late_tile = tile_scatter(m_threethree[None], rows, cols)
    inverse_three = (
        -(sum_three - product(sum_one, coupled[1]) + product(inverse_two, coupled[2]))
        * keep_three
    )
    own_tile = early_tile.at[2].add(late_tile[0])
    return (inverse_one, inverse_two, inverse_three, own_tile)


def solution(mesh):
    in_specs = (
        P("row", "col"),
        P(("row", "col"), None),
        P(("row", "col"), None),
        P(("row", "col"), None),
        P(),
        P(),
        P(),
        P(),
    )
    out_specs = (
        P(("row", "col"), None),
        P(("row", "col"), None),
        P(("row", "col"), None),
        P(None, "row", "col"),
    )
    local = functools.partial(body, mesh.shape["row"], mesh.shape["col"])
    return jax.shard_map(local, mesh=mesh, in_specs=in_specs, out_specs=out_specs, check_vma=False)
```

```python
import functools

import jax
import jax.numpy as jnp
from jax import lax
from jax.experimental import pallas as pl
from jax.experimental.pallas import tpu as pltpu
from jax.sharding import PartitionSpec as P

F32 = jnp.float32
BF16 = jnp.bfloat16
F16 = jnp.float16
SCALE = 32.0
LITTLE = pl.CostEstimate(flops=1, bytes_accessed=1, transcendentals=0)


def product(former, latter):
    return jnp.dot(
        former, latter, precision=lax.Precision.HIGHEST, preferred_element_type=F32
    )


def piece_keep(listed, start_row, slab_rows, block_width):
    rows_here = start_row + jnp.arange(slab_rows, dtype=jnp.int32)
    matches = (rows_here // block_width)[:, None] == listed[None, :]
    return jnp.any(matches, axis=1).astype(F32)[:, None]


def spread_step(own, step, rows, cols):
    ratio = cols // rows
    pairs = []
    for plane in range(rows):
        for place in range(cols):
            target = ((place % rows) ^ step) * cols + plane * ratio + place // rows
            pairs.append((plane * cols + place, target))
    return lax.ppermute(own, ("row", "col"), pairs)


def spread_panel(own, rows, cols):
    return [spread_step(own, step, rows, cols) for step in range(rows)]


def split_dot(former, latter, dims):
    high = former.astype(BF16)
    low = (former - high.astype(F32)).astype(BF16)
    dims = (dims, ((), ()))
    return lax.dot_general(high, latter, dims, preferred_element_type=F32) + lax.dot_general(
        low, latter, dims, preferred_element_type=F32
    )


def join_kernel(*refs):
    span = refs[0].shape[1]
    for index, panel_ref in enumerate(refs[:-1]):
        refs[-1][:, index * span : (index + 1) * span] = panel_ref[...]


def join(panels):
    rows, span = panels[0].shape
    whole = pl.BlockSpec(memory_space=pltpu.VMEM)
    return pl.pallas_call(
        join_kernel,
        in_specs=[whole] * len(panels),
        out_specs=whole,
        out_shape=jax.ShapeDtypeStruct((rows, span * len(panels)), panels[0].dtype),
        cost_estimate=LITTLE,
    )(*panels)


def kept(keeps, panel, row, span, value):
    return jnp.where(keeps[panel, row // span] > 0, value, jnp.zeros_like(value))


def multiply_kernel(where, keeps, s_ref, *refs, depth, span):
    pieces, out_ref, panel = refs[:-2], refs[-2], refs[-1]

    @pl.when(pl.program_id(0) == 0)
    def _():
        unit = min(depth, span)
        for step, piece in enumerate(pieces):
            begin = (where[0] ^ step) * depth
            for part in range(0, depth, unit):
                target = pl.ds(pl.multiple_of(begin + part, unit), unit)
                for index in range(panel.shape[1] // span):
                    lanes = slice(index * span, (index + 1) * span)
                    panel[target, lanes] = kept(
                        keeps, index, where[3] + begin + part, span, piece[part : part + unit, lanes]
                    )

    out_ref[0] = split_dot(s_ref[...], panel[...], ((1,), (0,)))


def multiply(where, keeps, ancestor, pieces, span):
    local_rows, local_cols = ancestor.shape
    slab_rows, width = pieces[0].shape
    chips = local_rows // slab_rows // 2
    return pl.pallas_call(
        functools.partial(multiply_kernel, depth=slab_rows, span=span),
        grid_spec=pltpu.PrefetchScalarGridSpec(
            num_scalar_prefetch=2,
            grid=(chips,),
            in_specs=[
                pl.BlockSpec((slab_rows, local_cols), lambda i, where, keeps: (2 * i + where[1], 0))
            ]
            + [pl.BlockSpec(piece.shape, lambda *at: (0, 0)) for piece in pieces],
            out_specs=pl.BlockSpec((1, slab_rows, width), lambda i, *at: (i, 0, 0)),
            scratch_shapes=[pltpu.VMEM((local_cols, width), BF16)],
        ),
        out_shape=jax.ShapeDtypeStruct((chips, slab_rows, width), F32),
        compiler_params=pltpu.CompilerParams(vmem_limit_bytes=34 * 1024 * 1024),
        cost_estimate=LITTLE,
    )(where, keeps, ancestor, *pieces)


def sum_kernel(where, mine_ref, handed_ref, own_ref, sent_ref):
    step = pl.program_id(0)
    summed = mine_ref[0] + handed_ref[0]

    @pl.when(step == 0)
    def _():
        own_ref[...] = summed

    @pl.when(step > 0)
    def _():
        sent_ref[0] = summed * SCALE


def chip_sum(where, mine, handed):
    chips, depth, width = mine.shape
    taken = pl.BlockSpec((1, depth, width), lambda i, where: (where[2] ^ i, 0, 0))
    return pl.pallas_call(
        sum_kernel,
        grid_spec=pltpu.PrefetchScalarGridSpec(
            num_scalar_prefetch=1,
            grid=(chips,),
            in_specs=[taken, taken],
            out_specs=[
                pl.BlockSpec((depth, width), lambda *at: (0, 0)),
                pl.BlockSpec((1, depth, width), lambda i, *at: (jnp.maximum(i - 1, 0), 0, 0)),
            ],
        ),
        out_shape=[
            jax.ShapeDtypeStruct((depth, width), F32),
            jax.ShapeDtypeStruct((chips - 1, depth, width), F32),
        ],
        compiler_params=pltpu.CompilerParams(vmem_limit_bytes=24 * 1024 * 1024),
        cost_estimate=LITTLE,
    )(where, mine, handed)


def sibling(value, cols):
    return lax.ppermute(value, "col", [(c, c ^ 1) for c in range(cols)])


def to_chip(value, step, cols):
    return lax.ppermute(value, "col", [(c, c ^ (2 * step)) for c in range(cols)])


def after(value, others):
    return lax.optimization_barrier((value, others))[0]


def take(pieces, index):
    return lax.dynamic_index_in_dim(pieces, index, 0, keepdims=False)


def chip_scatter(summed, cols):
    chip = lax.axis_index("col") // 2
    total = take(summed, chip)
    arrived = [to_chip(take(summed, chip ^ step), step, cols) for step in range(1, cols // 2)]
    for piece in arrived:
        total = total + piece
    return total


def hand_over(payloads, cols):
    return [to_chip(payload, step + 1, cols) for step, payload in enumerate(payloads)]


def collect(own, arrived):
    total = own
    for payload in arrived:
        total = total + payload.astype(F32) * (1.0 / SCALE)
    return total


def small_kernel(where, keeps, sums, rows, couple, ends, out_ref):
    start, inner = ((0,), (0,)), ((1,), (0,))
    c_zero, c_one, c_two = couple[0], couple[1], couple[2]
    width = c_zero.shape[0]
    depth = rows.shape[0]
    unit = min(depth, width)

    def end(index):
        return jnp.where(where[4] == 0, ends[index], jnp.zeros_like(ends[index]))

    def turned(left, right):
        return split_dot(right, left, start).T

    def block(j, i):
        total = jnp.zeros((width, width), F32)
        for part in range(0, depth, unit):
            here = slice(part, part + unit)
            factor = rows[here, i * width : (i + 1) * width]
            factor = kept(keeps, i, where[4] + part, width, factor)
            total += split_dot(sums[here, j * width : (j + 1) * width], factor, start)
        return total

    t_oneone, t_twoone, t_threeone = block(0, 0), block(0, 1), block(0, 2)
    t_twotwo, t_threetwo, t_threethree = block(1, 1), block(1, 2), block(2, 2)
    m_twoone, m_threeone = t_twoone.T, t_threeone.T
    diag_one = end(0) + t_oneone.T
    cross_two = t_twoone - split_dot(diag_one, c_zero, inner)
    diag_two = (
        end(1) + t_twotwo.T - split_dot(m_twoone, c_zero, inner) - turned(c_zero, cross_two)
    )
    second_three = t_threetwo.T - split_dot(m_threeone, c_zero, inner)
    cross_first = t_threeone - split_dot(diag_one, c_one, inner) - split_dot(cross_two, c_two, inner)
    cross_second = (
        second_three.T
        - split_dot(cross_two, c_one, start)
        - split_dot(diag_two, c_two, inner)
    )
    diag_three = (
        end(2)
        + t_threethree.T
        - split_dot(m_threeone, c_one, inner)
        - split_dot(second_three, c_two, inner)
        - turned(c_one, cross_first)
        - turned(c_two, cross_second)
    )
    part = out_ref.shape[3]
    blocks = (diag_one, diag_two, diag_three, cross_two, cross_first, cross_second)
    for index, value in enumerate(blocks):
        value = value.T
        for place in range(width // part):
            out_ref[place % 2, place // 2, index] = value[place * part : (place + 1) * part, :]


def small_parts(where, keeps, sums, rows, couplings, ends, cols):
    width = couplings.shape[1]
    whole = pl.BlockSpec(memory_space=pltpu.VMEM)
    scalars = pl.BlockSpec(memory_space=pltpu.SMEM)
    return pl.pallas_call(
        small_kernel,
        in_specs=[scalars] * 2 + [whole] * 4,
        out_specs=whole,
        out_shape=jax.ShapeDtypeStruct((2, cols // 2, 6, width // cols, width), F32),
        compiler_params=pltpu.CompilerParams(vmem_limit_bytes=24 * 1024 * 1024),
        cost_estimate=LITTLE,
    )(where, keeps, sums, rows, couplings, ends)


def tile_scatter(split, rows, cols):
    row, core, chip = lax.axis_index("row"), lax.axis_index("col") % 2, lax.axis_index("col") // 2
    held = take(split, core) + sibling(take(split, 1 - core), cols)
    bit = cols // 4
    while bit:
        halves = held.reshape(2, bit, *held.shape[1:])
        side = chip // bit % 2
        held = take(halves, side) + to_chip(take(halves, 1 - side), bit, cols)
        bit //= 2
    held = held[0]
    bit = rows // 2
    while bit:
        size = held.shape[2] // 2
        side = row // bit % 2
        mine = lax.dynamic_slice_in_dim(held, side * size, size, 2)
        theirs = lax.dynamic_slice_in_dim(held, (1 - side) * size, size, 2)
        pairs = [(r, r ^ bit) for r in range(rows)]
        held = mine + lax.ppermute(theirs, "row", pairs)
        bit //= 2
    return jnp.swapaxes(held, 1, 2)


def body(
    rows,
    cols,
    ancestor,
    panel_one,
    panel_two,
    panel_three,
    couplings,
    diag_terms,
    list_two,
    list_three,
):
    block_width = couplings.shape[1]
    slab_rows = panel_one.shape[0]
    row_id, col_id = lax.axis_index("row"), lax.axis_index("col")
    device = row_id * cols + col_id
    core, chip = col_id % 2, col_id // 2
    others = [chip, col_id * ancestor.shape[1], device * slab_rows]
    where = jnp.stack([row_id, core] + others).astype(jnp.int32)
    other_where = jnp.stack([row_id, 1 - core] + others).astype(jnp.int32)
    keep_two = piece_keep(list_two, device * slab_rows, slab_rows, block_width)
    keep_three = piece_keep(list_three, device * slab_rows, slab_rows, block_width)
    blocks = jnp.arange(ancestor.shape[0] * rows // block_width, dtype=jnp.int32)
    listed_two = jnp.any(blocks[:, None] == list_two[None, :], axis=1)
    listed_three = jnp.any(blocks[:, None] == list_three[None, :], axis=1)
    keeps = jnp.stack([jnp.ones_like(listed_two), listed_two, listed_three]).astype(jnp.int32)

    own_rows = join([panel_one, panel_two, panel_three])
    pieces = spread_panel(own_rows, rows, cols)
    theirs = multiply(other_where, keeps, ancestor, pieces, block_width)
    handed = sibling(theirs, cols)
    mine = multiply(after(where, theirs), keeps, ancestor, pieces, block_width)
    own, sent = chip_sum(where, mine, handed)
    payloads = [sent[step].astype(F16) for step in range(cols // 2 - 1)]
    total = collect(own, hand_over(payloads, cols))
    parts = small_parts(where, keeps, total, own_rows, couplings, diag_terms, cols)
    own_tile = tile_scatter(parts, rows, cols)
    sum_one = total[:, :block_width]
    sum_two = total[:, block_width : 2 * block_width]
    sum_three = total[:, 2 * block_width :]
    inverse_one = -sum_one
    coupled = couplings.astype(F32)
    inverse_two = -(sum_two - product(sum_one, coupled[0])) * keep_two
    known = product(sum_one, coupled[1]) - product(inverse_two, coupled[2])
    inverse_three = (known - sum_three) * keep_three
    return (inverse_one, inverse_two, inverse_three, own_tile)


def solution(mesh):
    in_specs = (
        P("row", "col"),
        P(("row", "col"), None),
        P(("row", "col"), None),
        P(("row", "col"), None),
        P(),
        P(),
        P(),
        P(),
    )
    out_specs = (
        P(("row", "col"), None),
        P(("row", "col"), None),
        P(("row", "col"), None),
        P(None, "row", "col"),
    )
    local = functools.partial(body, mesh.shape["row"], mesh.shape["col"])
    return jax.shard_map(local, mesh=mesh, in_specs=in_specs, out_specs=out_specs, check_vma=False)
```

```python
import functools

import jax
import jax.numpy as jnp
from jax import lax
from jax.experimental import pallas as pl
from jax.experimental.pallas import tpu as pltpu
from jax.sharding import PartitionSpec as P

F32 = jnp.float32
BF16 = jnp.bfloat16
F16 = jnp.float16
SCALE = 32.0
LITTLE = pl.CostEstimate(flops=1, bytes_accessed=1, transcendentals=0)


def product(former, latter):
    return jnp.dot(
        former, latter, precision=lax.Precision.HIGHEST, preferred_element_type=F32
    )


def piece_keep(listed, start_row, slab_rows, block_width):
    rows_here = start_row + jnp.arange(slab_rows, dtype=jnp.int32)
    matches = (rows_here // block_width)[:, None] == listed[None, :]
    return jnp.any(matches, axis=1).astype(F32)[:, None]


def swap_of(plane, rows):
    return plane % 2 * (rows // 2)


def spread_step(own, step, rows, cols):
    ratio = cols // rows
    pairs = []
    for plane in range(rows):
        for place in range(cols):
            to_plane = (place % rows) ^ step ^ swap_of(plane, rows)
            pairs.append((plane * cols + place, to_plane * cols + plane * ratio + place // rows))
    return lax.ppermute(own, ("row", "col"), pairs)


def spread(own, rows, cols):
    half = rows // 2
    early = [spread_step(own, step, rows, cols) for step in range(half)]
    late = [spread_step(after(own, early), half + step, rows, cols) for step in range(half)]
    return [(0, early)], [(half, late)]


def split_dot(former, latter, dims):
    high = former.astype(BF16)
    low = (former - high.astype(F32)).astype(BF16)
    dims = (dims, ((), ()))
    return lax.dot_general(high, latter, dims, preferred_element_type=F32) + lax.dot_general(
        low, latter, dims, preferred_element_type=F32
    )


def join_kernel(*refs):
    span = refs[0].shape[1]
    for index, panel_ref in enumerate(refs[:-1]):
        refs[-1][:, index * span : (index + 1) * span] = panel_ref[...]


def join(panels):
    rows, span = panels[0].shape
    whole = pl.BlockSpec(memory_space=pltpu.VMEM)
    return pl.pallas_call(
        join_kernel,
        in_specs=[whole] * len(panels),
        out_specs=whole,
        out_shape=jax.ShapeDtypeStruct((rows, span * len(panels)), panels[0].dtype),
        cost_estimate=LITTLE,
    )(*panels)


def kept(keeps, panel, row, span, value):
    return jnp.where(keeps[panel, row // span] > 0, value, jnp.zeros_like(value))


def multiply_kernel(where, keeps, *refs, depth, span, runs, kinds, added):
    s_refs, refs = refs[: len(runs)], refs[len(runs) :]
    panel = refs[-1]
    outs = refs[-1 - kinds : -1]

    @pl.when((pl.program_id(0) == 0) & (pl.program_id(1) == 0))
    def _():
        unit = min(depth, span)
        held = 0
        for first, count in runs:
            for step in range(count):
                piece = refs[held + step]
                place = where[0] ^ (first + step)
                for part in range(0, depth, unit):
                    begin = held * depth + place % count * depth + part
                    target = pl.ds(pl.multiple_of(begin, unit), unit)
                    row = where[3] + place * depth + part
                    for index in range(panel.shape[1] // span):
                        lanes = slice(index * span, (index + 1) * span)
                        value = piece[part : part + unit, lanes]
                        panel[target, lanes] = kept(keeps, index, row, span, value)
            held += count

    result = refs[-2 - kinds][0] if added else None
    begin = 0
    for s_ref in s_refs:
        end = begin + s_ref.shape[1]
        partial = split_dot(s_ref[...], panel[begin:end, :], ((1,), (0,)))
        result = partial if result is None else result + partial
        begin = end
    for kind, out_ref in enumerate(outs):

        @pl.when(pl.program_id(0) == kind)
        def _():
            out_ref[0] = result


def multiply(where, keeps, ancestor, runs, span, kinds, added=None):
    local_rows = ancestor.shape[0]
    pieces = [piece for _, run in runs for piece in run]
    slab_rows, width = pieces[0].shape
    chips = local_rows // slab_rows // 2

    def block_of(first, count):
        def at(h, i, where, keeps):
            kind = jnp.where(h == 0, where[1], 1 - where[1])
            return 2 * i + kind, (where[0] ^ first) // count

        return pl.BlockSpec((slab_rows, count * slab_rows), at)

    def out_at(kind):
        if kind == 0:
            return lambda h, i, *at: (jnp.where(h == 0, i, chips - 1), 0, 0)
        return lambda h, i, *at: (i * h, 0, 0)

    counts = tuple((first, len(run)) for first, run in runs)
    part = (1, slab_rows, width)
    extra = [] if added is None else [added]
    return pl.pallas_call(
        functools.partial(
            multiply_kernel,
            depth=slab_rows,
            span=span,
            runs=counts,
            kinds=kinds,
            added=len(extra),
        ),
        grid_spec=pltpu.PrefetchScalarGridSpec(
            num_scalar_prefetch=2,
            grid=(kinds, chips),
            in_specs=[block_of(*run) for run in counts]
            + [pl.BlockSpec(piece.shape, lambda *at: (0, 0)) for piece in pieces]
            + [pl.BlockSpec(part, out_at(0)) for _ in extra],
            out_specs=[pl.BlockSpec(part, out_at(kind)) for kind in range(kinds)],
            scratch_shapes=[pltpu.VMEM((len(pieces) * slab_rows, width), BF16)],
        ),
        out_shape=[jax.ShapeDtypeStruct((chips, slab_rows, width), F32)] * kinds,
        compiler_params=pltpu.CompilerParams(vmem_limit_bytes=34 * 1024 * 1024),
        cost_estimate=LITTLE,
    )(where, keeps, *([ancestor] * len(runs)), *pieces, *extra)


def sum_kernel(where, mine_ref, handed_ref, own_ref, sent_ref):
    step = pl.program_id(0)
    summed = mine_ref[0] + handed_ref[0]

    @pl.when(step == 0)
    def _():
        own_ref[...] = summed

    @pl.when(step > 0)
    def _():
        sent_ref[0] = summed * SCALE


def chip_sum(where, mine, handed):
    chips, depth, width = mine.shape
    taken = pl.BlockSpec((1, depth, width), lambda i, where: (where[2] ^ i, 0, 0))
    return pl.pallas_call(
        sum_kernel,
        grid_spec=pltpu.PrefetchScalarGridSpec(
            num_scalar_prefetch=1,
            grid=(chips,),
            in_specs=[taken, taken],
            out_specs=[
                pl.BlockSpec((depth, width), lambda *at: (0, 0)),
                pl.BlockSpec((1, depth, width), lambda i, *at: (jnp.maximum(i - 1, 0), 0, 0)),
            ],
        ),
        out_shape=[
            jax.ShapeDtypeStruct((depth, width), F32),
            jax.ShapeDtypeStruct((chips - 1, depth, width), F32),
        ],
        compiler_params=pltpu.CompilerParams(vmem_limit_bytes=24 * 1024 * 1024),
        cost_estimate=LITTLE,
    )(where, mine, handed)


def sibling(value, cols):
    return lax.ppermute(value, "col", [(c, c ^ 1) for c in range(cols)])


def to_chip(value, step, cols):
    return lax.ppermute(value, "col", [(c, c ^ (2 * step)) for c in range(cols)])


def after(value, others):
    return lax.optimization_barrier((value, others))[0]


def take(pieces, index):
    return lax.dynamic_index_in_dim(pieces, index, 0, keepdims=False)


def chip_scatter(summed, cols):
    chip = lax.axis_index("col") // 2
    total = take(summed, chip)
    arrived = [to_chip(take(summed, chip ^ step), step, cols) for step in range(1, cols // 2)]
    for piece in arrived:
        total = total + piece
    return total


def hand_over(payloads, cols):
    return [to_chip(payload, step + 1, cols) for step, payload in enumerate(payloads)]


def collect(own, arrived):
    total = own
    for payload in arrived:
        total = total + payload.astype(F32) * (1.0 / SCALE)
    return total


def small_kernel(where, keeps, sums, rows, couple, ends, out_ref):
    start, inner = ((0,), (0,)), ((1,), (0,))
    c_zero, c_one, c_two = couple[0], couple[1], couple[2]
    width = c_zero.shape[0]
    depth = rows.shape[0]
    unit = min(depth, width)

    def end(index):
        return jnp.where(where[4] == 0, ends[index], jnp.zeros_like(ends[index]))

    def turned(left, right):
        return split_dot(right, left, start).T

    def block(j, i):
        total = jnp.zeros((width, width), F32)
        for part in range(0, depth, unit):
            here = slice(part, part + unit)
            factor = rows[here, i * width : (i + 1) * width]
            factor = kept(keeps, i, where[4] + part, width, factor)
            total += split_dot(sums[here, j * width : (j + 1) * width], factor, start)
        return total

    t_oneone, t_twoone, t_threeone = block(0, 0), block(0, 1), block(0, 2)
    t_twotwo, t_threetwo, t_threethree = block(1, 1), block(1, 2), block(2, 2)
    m_twoone, m_threeone = t_twoone.T, t_threeone.T
    diag_one = end(0) + t_oneone.T
    cross_two = t_twoone - split_dot(diag_one, c_zero, inner)
    diag_two = (
        end(1) + t_twotwo.T - split_dot(m_twoone, c_zero, inner) - turned(c_zero, cross_two)
    )
    second_three = t_threetwo.T - split_dot(m_threeone, c_zero, inner)
    cross_first = t_threeone - split_dot(diag_one, c_one, inner) - split_dot(cross_two, c_two, inner)
    cross_second = (
        second_three.T
        - split_dot(cross_two, c_one, start)
        - split_dot(diag_two, c_two, inner)
    )
    diag_three = (
        end(2)
        + t_threethree.T
        - split_dot(m_threeone, c_one, inner)
        - split_dot(second_three, c_two, inner)
        - turned(c_one, cross_first)
        - turned(c_two, cross_second)
    )
    part = out_ref.shape[3]
    blocks = (diag_one, diag_two, diag_three, cross_two, cross_first, cross_second)
    for index, value in enumerate(blocks):
        value = value.T
        for place in range(width // part):
            out_ref[place % 2, place // 2, index] = value[place * part : (place + 1) * part, :]


def small_parts(where, keeps, sums, rows, couplings, ends, cols):
    width = couplings.shape[1]
    whole = pl.BlockSpec(memory_space=pltpu.VMEM)
    scalars = pl.BlockSpec(memory_space=pltpu.SMEM)
    return pl.pallas_call(
        small_kernel,
        in_specs=[scalars] * 2 + [whole] * 4,
        out_specs=whole,
        out_shape=jax.ShapeDtypeStruct((2, cols // 2, 6, width // cols, width), F32),
        compiler_params=pltpu.CompilerParams(vmem_limit_bytes=24 * 1024 * 1024),
        cost_estimate=LITTLE,
    )(where, keeps, sums, rows, couplings, ends)


def tile_scatter(split, rows, cols):
    row, core, chip = lax.axis_index("row"), lax.axis_index("col") % 2, lax.axis_index("col") // 2
    held = take(split, core) + sibling(take(split, 1 - core), cols)
    arrived = [to_chip(take(held, chip ^ step), step, cols) for step in range(1, cols // 2)]
    held = functools.reduce(jnp.add, arrived, take(held, chip))
    bit = rows // 2
    while bit:
        size = held.shape[2] // 2
        side = row // bit % 2
        mine = lax.dynamic_slice_in_dim(held, side * size, size, 2)
        theirs = lax.dynamic_slice_in_dim(held, (1 - side) * size, size, 2)
        pairs = [(r, r ^ bit) for r in range(rows)]
        held = mine + lax.ppermute(theirs, "row", pairs)
        bit //= 2
    return jnp.swapaxes(held, 1, 2)


def body(
    rows,
    cols,
    ancestor,
    panel_one,
    panel_two,
    panel_three,
    couplings,
    diag_terms,
    list_two,
    list_three,
):
    block_width = couplings.shape[1]
    slab_rows = panel_one.shape[0]
    row_id, col_id = lax.axis_index("row"), lax.axis_index("col")
    device = row_id * cols + col_id
    core, chip = col_id % 2, col_id // 2
    others = [chip, col_id * ancestor.shape[1], device * slab_rows]
    turned_row = row_id ^ swap_of(col_id // (cols // rows), rows)
    where = jnp.stack([turned_row, core] + others).astype(jnp.int32)
    other_where = jnp.stack([turned_row, 1 - core] + others).astype(jnp.int32)
    keep_two = piece_keep(list_two, device * slab_rows, slab_rows, block_width)
    keep_three = piece_keep(list_three, device * slab_rows, slab_rows, block_width)
    blocks = jnp.arange(ancestor.shape[0] * rows // block_width, dtype=jnp.int32)
    listed_two = jnp.any(blocks[:, None] == list_two[None, :], axis=1)
    listed_three = jnp.any(blocks[:, None] == list_three[None, :], axis=1)
    keeps = jnp.stack([jnp.ones_like(listed_two), listed_two, listed_three]).astype(jnp.int32)

    own_rows = join([panel_one, panel_two, panel_three])
    early, late = spread(own_rows, rows, cols)
    shared = (keeps, ancestor)
    theirs, mine = multiply(other_where, *shared, early, block_width, 2)
    (theirs,) = multiply(other_where, *shared, late, block_width, 1, theirs)
    handed = sibling(theirs, cols)
    turn = after(where, theirs)
    (mine,) = multiply(turn, *shared, late, block_width, 1, mine)
    own, sent = chip_sum(where, mine, handed)
    payloads = [sent[step].astype(F16) for step in range(cols // 2 - 1)]
    total = collect(own, hand_over(payloads, cols))
    parts = small_parts(where, keeps, total, own_rows, couplings, diag_terms, cols)
    own_tile = tile_scatter(parts, rows, cols)
    sum_one = total[:, :block_width]
    sum_two = total[:, block_width : 2 * block_width]
    sum_three = total[:, 2 * block_width :]
    inverse_one = -sum_one
    coupled = couplings.astype(F32)
    inverse_two = -(sum_two - product(sum_one, coupled[0])) * keep_two
    known = product(sum_one, coupled[1]) - product(inverse_two, coupled[2])
    inverse_three = (known - sum_three) * keep_three
    return (inverse_one, inverse_two, inverse_three, own_tile)


def solution(mesh):
    in_specs = (
        P("row", "col"),
        P(("row", "col"), None),
        P(("row", "col"), None),
        P(("row", "col"), None),
        P(),
        P(),
        P(),
        P(),
    )
    out_specs = (
        P(("row", "col"), None),
        P(("row", "col"), None),
        P(("row", "col"), None),
        P(None, "row", "col"),
    )
    local = functools.partial(body, mesh.shape["row"], mesh.shape["col"])
    return jax.shard_map(local, mesh=mesh, in_specs=in_specs, out_specs=out_specs, check_vma=False)
```

```python
import functools

import jax
import jax.numpy as jnp
from jax import lax
from jax.experimental import pallas as pl
from jax.experimental.pallas import tpu as pltpu
from jax.sharding import PartitionSpec as P

F32 = jnp.float32
BF16 = jnp.bfloat16
F16 = jnp.float16
SCALE = 32.0
LITTLE = pl.CostEstimate(flops=1, bytes_accessed=1, transcendentals=0)


def product(former, latter):
    return jnp.dot(
        former, latter, precision=lax.Precision.HIGHEST, preferred_element_type=F32
    )


def piece_keep(listed, start_row, slab_rows, block_width):
    rows_here = start_row + jnp.arange(slab_rows, dtype=jnp.int32)
    matches = (rows_here // block_width)[:, None] == listed[None, :]
    return jnp.any(matches, axis=1).astype(F32)[:, None]


def swap_of(plane, rows):
    return plane % 2 * (rows // 2)


def spread_step(own, step, rows, cols):
    ratio = cols // rows
    pairs = []
    for plane in range(rows):
        for place in range(cols):
            to_plane = (place % rows) ^ step ^ swap_of(plane, rows)
            pairs.append((plane * cols + place, to_plane * cols + plane * ratio + place // rows))
    return lax.ppermute(own, ("row", "col"), pairs)


def spread(own, rows, cols):
    half = rows // 2
    early = [spread_step(own, step, rows, cols) for step in range(half)]
    late = [spread_step(after(own, early), half + step, rows, cols) for step in range(half)]
    return (0, early), (half, late)


def split_dot(former, latter, dims):
    high = former.astype(BF16)
    low = (former - high.astype(F32)).astype(BF16)
    dims = (dims, ((), ()))
    return lax.dot_general(high, latter, dims, preferred_element_type=F32) + lax.dot_general(
        low, latter, dims, preferred_element_type=F32
    )


def join_kernel(*refs):
    span = refs[0].shape[1]
    for index, panel_ref in enumerate(refs[:-1]):
        refs[-1][:, index * span : (index + 1) * span] = panel_ref[...]


def join(panels):
    rows, span = panels[0].shape
    whole = pl.BlockSpec(memory_space=pltpu.VMEM)
    return pl.pallas_call(
        join_kernel,
        in_specs=[whole] * len(panels),
        out_specs=whole,
        out_shape=jax.ShapeDtypeStruct((rows, span * len(panels)), panels[0].dtype),
        cost_estimate=LITTLE,
    )(*panels)


def kept(keeps, panel, row, span, value):
    return jnp.where(keeps[panel, row // span] > 0, value, jnp.zeros_like(value))


def multiply_kernel(where, keeps, s_ref, *refs, depth, span, first, count, added):
    out_ref, panel = refs[-2:]

    @pl.when((pl.program_id(0) == 0) & (pl.program_id(1) == 0))
    def _():
        unit = min(depth, span)
        for step in range(count):
            place = where[0] ^ (first + step)
            for part in range(0, depth, unit):
                target = pl.ds(pl.multiple_of(place % count * depth + part, unit), unit)
                row = where[3] + place * depth + part
                for index in range(panel.shape[1] // span):
                    lanes = slice(index * span, (index + 1) * span)
                    value = refs[step][part : part + unit, lanes]
                    panel[target, lanes] = kept(keeps, index, row, span, value)

    result = split_dot(s_ref[...], panel[...], ((1,), (0,)))
    if added:
        result += refs[count][0, 0]
    out_ref[0, 0] = result


def multiply(where, keeps, ancestor, run, span, kinds, added=None):
    first, pieces = run
    count = len(pieces)
    slab_rows, width = pieces[0].shape
    chips = ancestor.shape[0] // slab_rows // 2
    base = kinds[0]

    def rows_at(h, i, where, keeps):
        kind = jnp.where(h + base == 1, where[1], 1 - where[1])
        return 2 * i + kind, (where[0] ^ first) // count

    extra = [] if added is None else [added]
    part = (1, 1, slab_rows, width)
    return pl.pallas_call(
        functools.partial(
            multiply_kernel,
            depth=slab_rows,
            span=span,
            first=first,
            count=count,
            added=len(extra),
        ),
        grid_spec=pltpu.PrefetchScalarGridSpec(
            num_scalar_prefetch=2,
            grid=(len(kinds), chips),
            in_specs=[pl.BlockSpec((slab_rows, count * slab_rows), rows_at)]
            + [pl.BlockSpec(piece.shape, lambda *at: (0, 0)) for piece in pieces]
            + [pl.BlockSpec(part, lambda h, i, *at: (h + base, i, 0, 0)) for _ in extra],
            out_specs=pl.BlockSpec(part, lambda h, i, *at: (h, i, 0, 0)),
            scratch_shapes=[pltpu.VMEM((count * slab_rows, width), BF16)],
        ),
        out_shape=jax.ShapeDtypeStruct((len(kinds), chips, slab_rows, width), F32),
        compiler_params=pltpu.CompilerParams(vmem_limit_bytes=21 * 1024 * 1024),
        cost_estimate=LITTLE,
    )(where, keeps, ancestor, *pieces, *extra)


def sum_kernel(where, mine_ref, handed_ref, own_ref, sent_ref):
    step = pl.program_id(0)
    summed = mine_ref[0, 0] + handed_ref[0, 0]

    @pl.when(step == 0)
    def _():
        own_ref[...] = summed

    @pl.when(step > 0)
    def _():
        sent_ref[0] = summed * SCALE


def chip_sum(where, mine, handed):
    chips, depth, width = mine.shape[1:]
    taken = pl.BlockSpec((1, 1, depth, width), lambda i, where: (0, where[2] ^ i, 0, 0))
    return pl.pallas_call(
        sum_kernel,
        grid_spec=pltpu.PrefetchScalarGridSpec(
            num_scalar_prefetch=1,
            grid=(chips,),
            in_specs=[taken, taken],
            out_specs=[
                pl.BlockSpec((depth, width), lambda *at: (0, 0)),
                pl.BlockSpec((1, depth, width), lambda i, *at: (jnp.maximum(i - 1, 0), 0, 0)),
            ],
        ),
        out_shape=[
            jax.ShapeDtypeStruct((depth, width), F32),
            jax.ShapeDtypeStruct((chips - 1, depth, width), F32),
        ],
        compiler_params=pltpu.CompilerParams(vmem_limit_bytes=14 * 1024 * 1024),
        cost_estimate=LITTLE,
    )(where, mine, handed)


def sibling(value, cols):
    return lax.ppermute(value, "col", [(c, c ^ 1) for c in range(cols)])


def to_chip(value, step, cols):
    return lax.ppermute(value, "col", [(c, c ^ (2 * step)) for c in range(cols)])


def after(value, others):
    return lax.optimization_barrier((value, others))[0]


def take(pieces, index):
    return lax.dynamic_index_in_dim(pieces, index, 0, keepdims=False)


def chip_scatter(summed, cols):
    chip = lax.axis_index("col") // 2
    total = take(summed, chip)
    arrived = [to_chip(take(summed, chip ^ step), step, cols) for step in range(1, cols // 2)]
    for piece in arrived:
        total = total + piece
    return total


def hand_over(payloads, cols):
    return [to_chip(payload, step + 1, cols) for step, payload in enumerate(payloads)]


def collect(own, arrived):
    total = own
    for payload in arrived:
        total = total + payload.astype(F32) * (1.0 / SCALE)
    return total


def small_kernel(where, keeps, sums, rows, couple, ends, stay_ref, give_ref):
    start, inner = ((0,), (0,)), ((1,), (0,))
    c_zero, c_one, c_two = couple[0], couple[1], couple[2]
    width = c_zero.shape[0]
    depth = rows.shape[0]
    unit = min(depth, width)

    def end(index):
        return jnp.where(where[4] == 0, ends[index], jnp.zeros_like(ends[index]))

    def turned(left, right):
        return split_dot(right, left, start).T

    def block(j, i):
        total = jnp.zeros((width, width), F32)
        for part in range(0, depth, unit):
            here = slice(part, part + unit)
            factor = rows[here, i * width : (i + 1) * width]
            factor = kept(keeps, i, where[4] + part, width, factor)
            total += split_dot(sums[here, j * width : (j + 1) * width], factor, start)
        return total

    t_oneone, t_twoone, t_threeone = block(0, 0), block(0, 1), block(0, 2)
    t_twotwo, t_threetwo, t_threethree = block(1, 1), block(1, 2), block(2, 2)
    m_twoone, m_threeone = t_twoone.T, t_threeone.T
    diag_one = end(0) + t_oneone.T
    cross_two = t_twoone - split_dot(diag_one, c_zero, inner)
    diag_two = (
        end(1) + t_twotwo.T - split_dot(m_twoone, c_zero, inner) - turned(c_zero, cross_two)
    )
    second_three = t_threetwo.T - split_dot(m_threeone, c_zero, inner)
    cross_first = t_threeone - split_dot(diag_one, c_one, inner) - split_dot(cross_two, c_two, inner)
    cross_second = (
        second_three.T
        - split_dot(cross_two, c_one, start)
        - split_dot(diag_two, c_two, inner)
    )
    diag_three = (
        end(2)
        + t_threethree.T
        - split_dot(m_threeone, c_one, inner)
        - split_dot(second_three, c_two, inner)
        - turned(c_one, cross_first)
        - turned(c_two, cross_second)
    )
    part = stay_ref.shape[2]
    blocks = (diag_one, diag_two, diag_three, cross_two, cross_first, cross_second)
    for index, value in enumerate(blocks):
        value = value.T
        for place in range(width // part):
            strip = value[place * part : (place + 1) * part, :]

            @pl.when(where[1] == place % 2)
            def _():
                stay_ref[place // 2, index] = strip

            @pl.when(where[1] != place % 2)
            def _():
                give_ref[place // 2, index] = strip


def small_parts(where, keeps, sums, rows, couplings, ends, cols):
    width = couplings.shape[1]
    whole = pl.BlockSpec(memory_space=pltpu.VMEM)
    scalars = pl.BlockSpec(memory_space=pltpu.SMEM)
    return pl.pallas_call(
        small_kernel,
        in_specs=[scalars] * 2 + [whole] * 4,
        out_specs=[whole] * 2,
        out_shape=[jax.ShapeDtypeStruct((cols // 2, 6, width // cols, width), F32)] * 2,
        compiler_params=pltpu.CompilerParams(vmem_limit_bytes=16 * 1024 * 1024),
        cost_estimate=LITTLE,
    )(where, keeps, sums, rows, couplings, ends)


def tile_scatter(stay, give, rows, cols):
    row, chip = lax.axis_index("row"), lax.axis_index("col") // 2
    held = stay + sibling(give, cols)
    arrived = [to_chip(take(held, chip ^ step), step, cols) for step in range(1, cols // 2)]
    held = functools.reduce(jnp.add, arrived, take(held, chip))
    bit = rows // 2
    while bit:
        size = held.shape[2] // 2
        side = row // bit % 2
        mine = lax.dynamic_slice_in_dim(held, side * size, size, 2)
        theirs = lax.dynamic_slice_in_dim(held, (1 - side) * size, size, 2)
        pairs = [(r, r ^ bit) for r in range(rows)]
        held = mine + lax.ppermute(theirs, "row", pairs)
        bit //= 2
    return jnp.swapaxes(held, 1, 2)


def body(
    rows,
    cols,
    ancestor,
    panel_one,
    panel_two,
    panel_three,
    couplings,
    diag_terms,
    list_two,
    list_three,
):
    block_width = couplings.shape[1]
    slab_rows = panel_one.shape[0]
    row_id, col_id = lax.axis_index("row"), lax.axis_index("col")
    device = row_id * cols + col_id
    core, chip = col_id % 2, col_id // 2
    others = [chip, col_id * ancestor.shape[1], device * slab_rows]
    turned_row = row_id ^ swap_of(col_id // (cols // rows), rows)
    where = jnp.stack([turned_row, core] + others).astype(jnp.int32)
    keep_two = piece_keep(list_two, device * slab_rows, slab_rows, block_width)
    keep_three = piece_keep(list_three, device * slab_rows, slab_rows, block_width)
    blocks = jnp.arange(ancestor.shape[0] * rows // block_width, dtype=jnp.int32)
    listed_two = jnp.any(blocks[:, None] == list_two[None, :], axis=1)
    listed_three = jnp.any(blocks[:, None] == list_three[None, :], axis=1)
    keeps = jnp.stack([jnp.ones_like(listed_two), listed_two, listed_three]).astype(jnp.int32)

    own_rows = join([panel_one, panel_two, panel_three])
    early, late = spread(own_rows, rows, cols)
    sums = multiply(where, keeps, ancestor, early, block_width, (0, 1))
    theirs = multiply(where, keeps, ancestor, late, block_width, (0,), sums)
    handed = sibling(theirs, cols)
    turn = after(where, theirs)
    mine = multiply(turn, keeps, ancestor, late, block_width, (1,), sums)
    own, sent = chip_sum(where, mine, handed)
    payloads = [sent[step].astype(F16) for step in range(cols // 2 - 1)]
    total = collect(own, hand_over(payloads, cols))
    parts = small_parts(where, keeps, total, own_rows, couplings, diag_terms, cols)
    own_tile = tile_scatter(*parts, rows, cols)
    sum_one = total[:, :block_width]
    sum_two = total[:, block_width : 2 * block_width]
    sum_three = total[:, 2 * block_width :]
    inverse_one = -sum_one
    coupled = couplings.astype(F32)
    inverse_two = -(sum_two - product(sum_one, coupled[0])) * keep_two
    known = product(sum_one, coupled[1]) - product(inverse_two, coupled[2])
    inverse_three = (known - sum_three) * keep_three
    return (inverse_one, inverse_two, inverse_three, own_tile)


def solution(mesh):
    in_specs = (
        P("row", "col"),
        P(("row", "col"), None),
        P(("row", "col"), None),
        P(("row", "col"), None),
        P(),
        P(),
        P(),
        P(),
    )
    out_specs = (
        P(("row", "col"), None),
        P(("row", "col"), None),
        P(("row", "col"), None),
        P(None, "row", "col"),
    )
    local = functools.partial(body, mesh.shape["row"], mesh.shape["col"])
    return jax.shard_map(local, mesh=mesh, in_specs=in_specs, out_specs=out_specs, check_vma=False)
```

```python
import functools

import jax
import jax.numpy as jnp
from jax import lax
from jax.experimental import pallas as pl
from jax.experimental.pallas import tpu as pltpu
from jax.sharding import PartitionSpec as P

F32 = jnp.float32
BF16 = jnp.bfloat16
F16 = jnp.float16
TOP = 2.0**15
FLOOR = 2.0**-14
SUBLANES = 8
TAIL = 16
LITTLE = pl.CostEstimate(flops=1, bytes_accessed=1, transcendentals=0)


def product(former, latter):
    return jnp.dot(
        former, latter, precision=lax.Precision.HIGHEST, preferred_element_type=F32
    )


def piece_keep(listed, start_row, slab_rows, block_width):
    rows_here = start_row + jnp.arange(slab_rows, dtype=jnp.int32)
    matches = (rows_here // block_width)[:, None] == listed[None, :]
    return jnp.any(matches, axis=1).astype(F32)[:, None]


def swap_of(plane, rows):
    return plane % 2 * (rows // 2)


def spread_step(own, step, rows, cols):
    ratio = cols // rows
    pairs = []
    for plane in range(rows):
        for place in range(cols):
            to_plane = (place % rows) ^ step ^ swap_of(plane, rows)
            pairs.append((plane * cols + place, to_plane * cols + plane * ratio + place // rows))
    return lax.ppermute(own, ("row", "col"), pairs)


def spread(own, rows, cols):
    half = rows // 2
    early = [spread_step(own, step, rows, cols) for step in range(half)]
    late = [spread_step(after(own, early), half + step, rows, cols) for step in range(half)]
    return (0, early), (half, late)


def split_dot(former, latter, dims):
    high = former.astype(BF16)
    low = (former - high.astype(F32)).astype(BF16)
    dims = (dims, ((), ()))
    return lax.dot_general(high, latter, dims, preferred_element_type=F32) + lax.dot_general(
        low, latter, dims, preferred_element_type=F32
    )


def join_kernel(*refs):
    span = refs[0].shape[1]
    for index, panel_ref in enumerate(refs[:-1]):
        refs[-1][:, index * span : (index + 1) * span] = panel_ref[...]


def join(panels):
    rows, span = panels[0].shape
    whole = pl.BlockSpec(memory_space=pltpu.VMEM)
    return pl.pallas_call(
        join_kernel,
        in_specs=[whole] * len(panels),
        out_specs=whole,
        out_shape=jax.ShapeDtypeStruct((rows, span * len(panels)), panels[0].dtype),
        cost_estimate=LITTLE,
    )(*panels)


def kept(keeps, panel, row, span, value):
    return jnp.where(keeps[panel, row // span] > 0, value, jnp.zeros_like(value))


def multiply_kernel(where, keeps, s_ref, *refs, depth, span, first, count, added):
    out_ref, panel = refs[-2:]

    @pl.when((pl.program_id(0) == 0) & (pl.program_id(1) == 0))
    def _():
        unit = min(depth, span)
        for step in range(count):
            place = where[0] ^ (first + step)
            for part in range(0, depth, unit):
                target = pl.ds(pl.multiple_of(place % count * depth + part, unit), unit)
                row = where[3] + place * depth + part
                for index in range(panel.shape[1] // span):
                    lanes = slice(index * span, (index + 1) * span)
                    value = refs[step][part : part + unit, lanes]
                    panel[target, lanes] = kept(keeps, index, row, span, value)

    result = split_dot(s_ref[...], panel[...], ((1,), (0,)))
    if added:
        result += refs[count][0, 0]
    out_ref[0, 0] = result


def multiply(where, keeps, ancestor, run, span, kinds, added=None):
    first, pieces = run
    count = len(pieces)
    slab_rows, width = pieces[0].shape
    chips = ancestor.shape[0] // slab_rows // 2
    base = kinds[0]

    def rows_at(h, i, where, keeps):
        kind = jnp.where(h + base == 1, where[1], 1 - where[1])
        return 2 * i + kind, (where[0] ^ first) // count

    extra = [] if added is None else [added]
    part = (1, 1, slab_rows, width)
    return pl.pallas_call(
        functools.partial(
            multiply_kernel,
            depth=slab_rows,
            span=span,
            first=first,
            count=count,
            added=len(extra),
        ),
        grid_spec=pltpu.PrefetchScalarGridSpec(
            num_scalar_prefetch=2,
            grid=(len(kinds), chips),
            in_specs=[pl.BlockSpec((slab_rows, count * slab_rows), rows_at)]
            + [pl.BlockSpec(piece.shape, lambda *at: (0, 0)) for piece in pieces]
            + [pl.BlockSpec(part, lambda h, i, *at: (h + base, i, 0, 0)) for _ in extra],
            out_specs=pl.BlockSpec(part, lambda h, i, *at: (h, i, 0, 0)),
            scratch_shapes=[pltpu.VMEM((count * slab_rows, width), BF16)],
        ),
        out_shape=jax.ShapeDtypeStruct((len(kinds), chips, slab_rows, width), F32),
        compiler_params=pltpu.CompilerParams(vmem_limit_bytes=21 * 1024 * 1024),
        cost_estimate=LITTLE,
    )(where, keeps, ancestor, *pieces, *extra)


def sum_kernel(where, mine_ref, handed_ref, own_ref, sent_ref):
    step = pl.program_id(0)
    summed = mine_ref[0, 0] + handed_ref[0, 0]
    depth, width = summed.shape

    @pl.when(step == 0)
    def _():
        own_ref[:depth, :] = summed
        own_ref[depth:, :] = jnp.zeros((TAIL, width), F32)

    @pl.when(step > 0)
    def _():
        most = jnp.max(jnp.abs(summed), axis=(0, 1), keepdims=True)
        unit = jnp.maximum(most, FLOOR).astype(BF16).astype(F32)
        sent_ref[0, :depth, :] = summed * (TOP / unit)
        sent_ref[0, depth:, :] = jnp.broadcast_to(unit, (TAIL, width))


def chip_sum(where, mine, handed):
    chips, depth, width = mine.shape[1:]
    taken = pl.BlockSpec((1, 1, depth, width), lambda i, where: (0, where[2] ^ i, 0, 0))
    longer = depth + TAIL
    return pl.pallas_call(
        sum_kernel,
        grid_spec=pltpu.PrefetchScalarGridSpec(
            num_scalar_prefetch=1,
            grid=(chips,),
            in_specs=[taken, taken],
            out_specs=[
                pl.BlockSpec((longer, width), lambda *at: (0, 0)),
                pl.BlockSpec((1, longer, width), lambda i, *at: (jnp.maximum(i - 1, 0), 0, 0)),
            ],
        ),
        out_shape=[
            jax.ShapeDtypeStruct((longer, width), F32),
            jax.ShapeDtypeStruct((chips - 1, longer, width), F32),
        ],
        compiler_params=pltpu.CompilerParams(vmem_limit_bytes=15 * 1024 * 1024),
        cost_estimate=LITTLE,
    )(where, mine, handed)


def sibling(value, cols):
    return lax.ppermute(value, "col", [(c, c ^ 1) for c in range(cols)])


def to_chip(value, step, cols):
    return lax.ppermute(value, "col", [(c, c ^ (2 * step)) for c in range(cols)])


def after(value, others):
    return lax.optimization_barrier((value, others))[0]


def take(pieces, index):
    return lax.dynamic_index_in_dim(pieces, index, 0, keepdims=False)


def chip_scatter(summed, cols):
    chip = lax.axis_index("col") // 2
    total = take(summed, chip)
    arrived = [to_chip(take(summed, chip ^ step), step, cols) for step in range(1, cols // 2)]
    for piece in arrived:
        total = total + piece
    return total


def hand_over(payloads, cols):
    return [to_chip(payload, step + 1, cols) for step, payload in enumerate(payloads)]


def collect(own, arrived):
    longer, width = own.shape
    groups = (longer // SUBLANES, SUBLANES, width)
    total = own.reshape(groups)
    for payload in arrived:
        unit = payload[longer - TAIL :].astype(F32)[:SUBLANES]
        total = total + payload.astype(F32).reshape(groups) * (unit * (1.0 / TOP))[None]
    return total.reshape(longer, width)


def small_kernel(where, keeps, sums, rows, couple, ends, stay_ref, give_ref):
    start, inner = ((0,), (0,)), ((1,), (0,))
    c_zero, c_one, c_two = couple[0], couple[1], couple[2]
    width = c_zero.shape[0]
    depth = rows.shape[0]
    unit = min(depth, width)

    def end(index):
        return jnp.where(where[4] == 0, ends[index], jnp.zeros_like(ends[index]))

    def turned(left, right):
        return split_dot(right, left, start).T

    def block(j, i):
        total = jnp.zeros((width, width), F32)
        for part in range(0, depth, unit):
            here = slice(part, part + unit)
            factor = rows[here, i * width : (i + 1) * width]
            factor = kept(keeps, i, where[4] + part, width, factor)
            total += split_dot(sums[here, j * width : (j + 1) * width], factor, start)
        return total

    t_oneone, t_twoone, t_threeone = block(0, 0), block(0, 1), block(0, 2)
    t_twotwo, t_threetwo, t_threethree = block(1, 1), block(1, 2), block(2, 2)
    m_twoone, m_threeone = t_twoone.T, t_threeone.T
    diag_one = end(0) + t_oneone.T
    cross_two = t_twoone - split_dot(diag_one, c_zero, inner)
    diag_two = (
        end(1) + t_twotwo.T - split_dot(m_twoone, c_zero, inner) - turned(c_zero, cross_two)
    )
    second_three = t_threetwo.T - split_dot(m_threeone, c_zero, inner)
    cross_first = t_threeone - split_dot(diag_one, c_one, inner) - split_dot(cross_two, c_two, inner)
    cross_second = (
        second_three.T
        - split_dot(cross_two, c_one, start)
        - split_dot(diag_two, c_two, inner)
    )
    diag_three = (
        end(2)
        + t_threethree.T
        - split_dot(m_threeone, c_one, inner)
        - split_dot(second_three, c_two, inner)
        - turned(c_one, cross_first)
        - turned(c_two, cross_second)
    )
    part = stay_ref.shape[2]
    blocks = (diag_one, diag_two, diag_three, cross_two, cross_first, cross_second)
    for index, value in enumerate(blocks):
        value = value.T
        for place in range(width // part):
            strip = value[place * part : (place + 1) * part, :]

            @pl.when(where[1] == place % 2)
            def _():
                stay_ref[place // 2, index] = strip

            @pl.when(where[1] != place % 2)
            def _():
                give_ref[place // 2, index] = strip


def small_parts(where, keeps, sums, rows, couplings, ends, cols):
    width = couplings.shape[1]
    whole = pl.BlockSpec(memory_space=pltpu.VMEM)
    scalars = pl.BlockSpec(memory_space=pltpu.SMEM)
    return pl.pallas_call(
        small_kernel,
        in_specs=[scalars] * 2 + [whole] * 4,
        out_specs=[whole] * 2,
        out_shape=[jax.ShapeDtypeStruct((cols // 2, 6, width // cols, width), F32)] * 2,
        compiler_params=pltpu.CompilerParams(vmem_limit_bytes=16 * 1024 * 1024),
        cost_estimate=LITTLE,
    )(where, keeps, sums, rows, couplings, ends)


def tile_scatter(stay, give, rows, cols):
    row, chip = lax.axis_index("row"), lax.axis_index("col") // 2
    held = stay + sibling(give, cols)
    arrived = [to_chip(take(held, chip ^ step), step, cols) for step in range(1, cols // 2)]
    held = functools.reduce(jnp.add, arrived, take(held, chip))
    bit = rows // 2
    while bit:
        size = held.shape[2] // 2
        side = row // bit % 2
        mine = lax.dynamic_slice_in_dim(held, side * size, size, 2)
        theirs = lax.dynamic_slice_in_dim(held, (1 - side) * size, size, 2)
        pairs = [(r, r ^ bit) for r in range(rows)]
        held = mine + lax.ppermute(theirs, "row", pairs)
        bit //= 2
    return jnp.swapaxes(held, 1, 2)


def body(
    rows,
    cols,
    ancestor,
    panel_one,
    panel_two,
    panel_three,
    couplings,
    diag_terms,
    list_two,
    list_three,
):
    block_width = couplings.shape[1]
    slab_rows = panel_one.shape[0]
    row_id, col_id = lax.axis_index("row"), lax.axis_index("col")
    device = row_id * cols + col_id
    core, chip = col_id % 2, col_id // 2
    others = [chip, col_id * ancestor.shape[1], device * slab_rows]
    turned_row = row_id ^ swap_of(col_id // (cols // rows), rows)
    where = jnp.stack([turned_row, core] + others).astype(jnp.int32)
    keep_two = piece_keep(list_two, device * slab_rows, slab_rows, block_width)
    keep_three = piece_keep(list_three, device * slab_rows, slab_rows, block_width)
    blocks = jnp.arange(ancestor.shape[0] * rows // block_width, dtype=jnp.int32)
    listed_two = jnp.any(blocks[:, None] == list_two[None, :], axis=1)
    listed_three = jnp.any(blocks[:, None] == list_three[None, :], axis=1)
    keeps = jnp.stack([jnp.ones_like(listed_two), listed_two, listed_three]).astype(jnp.int32)

    own_rows = join([panel_one, panel_two, panel_three])
    early, late = spread(own_rows, rows, cols)
    sums = multiply(where, keeps, ancestor, early, block_width, (0, 1))
    theirs = multiply(where, keeps, ancestor, late, block_width, (0,), sums)
    handed = sibling(theirs, cols)
    turn = after(where, theirs)
    mine = multiply(turn, keeps, ancestor, late, block_width, (1,), sums)
    own, sent = chip_sum(where, mine, handed)
    payloads = [sent[step].astype(F16) for step in range(cols // 2 - 1)]
    total = collect(own, hand_over(payloads, cols))
    parts = small_parts(where, keeps, total, own_rows, couplings, diag_terms, cols)
    own_tile = tile_scatter(*parts, rows, cols)
    sum_one = total[:slab_rows, :block_width]
    sum_two = total[:slab_rows, block_width : 2 * block_width]
    sum_three = total[:slab_rows, 2 * block_width :]
    inverse_one = -sum_one
    coupled = couplings.astype(F32)
    inverse_two = -(sum_two - product(sum_one, coupled[0])) * keep_two
    known = product(sum_one, coupled[1]) - product(inverse_two, coupled[2])
    inverse_three = (known - sum_three) * keep_three
    return (inverse_one, inverse_two, inverse_three, own_tile)


def solution(mesh):
    in_specs = (
        P("row", "col"),
        P(("row", "col"), None),
        P(("row", "col"), None),
        P(("row", "col"), None),
        P(),
        P(),
        P(),
        P(),
    )
    out_specs = (
        P(("row", "col"), None),
        P(("row", "col"), None),
        P(("row", "col"), None),
        P(None, "row", "col"),
    )
    local = functools.partial(body, mesh.shape["row"], mesh.shape["col"])
    return jax.shard_map(local, mesh=mesh, in_specs=in_specs, out_specs=out_specs, check_vma=False)
```

```python
import functools

import jax
import jax.numpy as jnp
from jax import lax
from jax.experimental import pallas as pl
from jax.experimental.pallas import tpu as pltpu
from jax.sharding import PartitionSpec as P

F32 = jnp.float32
BF16 = jnp.bfloat16
F16 = jnp.float16
TOP_POWER = 15.0
FLOOR = 2.0**-110
SUBLANES = 8
TAIL = 16
LITTLE = pl.CostEstimate(flops=1, bytes_accessed=1, transcendentals=0)


def product(former, latter):
    return jnp.dot(
        former, latter, precision=lax.Precision.HIGHEST, preferred_element_type=F32
    )


def piece_keep(listed, start_row, slab_rows, block_width):
    rows_here = start_row + jnp.arange(slab_rows, dtype=jnp.int32)
    matches = (rows_here // block_width)[:, None] == listed[None, :]
    return jnp.any(matches, axis=1).astype(F32)[:, None]


def swap_of(plane, rows):
    return plane % 2 * (rows // 2)


def spread_step(own, step, rows, cols):
    ratio = cols // rows
    pairs = []
    for plane in range(rows):
        for place in range(cols):
            to_plane = (place % rows) ^ step ^ swap_of(plane, rows)
            pairs.append((plane * cols + place, to_plane * cols + plane * ratio + place // rows))
    return lax.ppermute(own, ("row", "col"), pairs)


def spread(own, rows, cols):
    half = rows // 2
    early = [spread_step(own, step, rows, cols) for step in range(half)]
    late = [spread_step(after(own, early), half + step, rows, cols) for step in range(half)]
    return (0, early), (half, late)


def split_dot(former, latter, dims):
    high = former.astype(BF16)
    low = (former - high.astype(F32)).astype(BF16)
    dims = (dims, ((), ()))
    return lax.dot_general(high, latter, dims, preferred_element_type=F32) + lax.dot_general(
        low, latter, dims, preferred_element_type=F32
    )


def join_kernel(*refs):
    span = refs[0].shape[1]
    for index, panel_ref in enumerate(refs[:-1]):
        refs[-1][:, index * span : (index + 1) * span] = panel_ref[...]


def join(panels):
    rows, span = panels[0].shape
    whole = pl.BlockSpec(memory_space=pltpu.VMEM)
    return pl.pallas_call(
        join_kernel,
        in_specs=[whole] * len(panels),
        out_specs=whole,
        out_shape=jax.ShapeDtypeStruct((rows, span * len(panels)), panels[0].dtype),
        cost_estimate=LITTLE,
    )(*panels)


def kept(keeps, panel, row, span, value):
    return jnp.where(keeps[panel, row // span] > 0, value, jnp.zeros_like(value))


def multiply_kernel(where, keeps, s_ref, *refs, depth, span, first, count, added):
    out_ref, panel = refs[-2:]

    @pl.when((pl.program_id(0) == 0) & (pl.program_id(1) == 0))
    def _():
        unit = min(depth, span)
        for step in range(count):
            place = where[0] ^ (first + step)
            for part in range(0, depth, unit):
                target = pl.ds(pl.multiple_of(place % count * depth + part, unit), unit)
                row = where[3] + place * depth + part
                for index in range(panel.shape[1] // span):
                    lanes = slice(index * span, (index + 1) * span)
                    value = refs[step][part : part + unit, lanes]
                    panel[target, lanes] = kept(keeps, index, row, span, value)

    result = split_dot(s_ref[...], panel[...], ((1,), (0,)))
    if added:
        result += refs[count][0, 0]
    out_ref[0, 0] = result


def multiply(where, keeps, ancestor, run, span, kinds, added=None):
    first, pieces = run
    count = len(pieces)
    slab_rows, width = pieces[0].shape
    chips = ancestor.shape[0] // slab_rows // 2
    base = kinds[0]

    def rows_at(h, i, where, keeps):
        kind = jnp.where(h + base == 1, where[1], 1 - where[1])
        return 2 * i + kind, (where[0] ^ first) // count

    extra = [] if added is None else [added]
    part = (1, 1, slab_rows, width)
    return pl.pallas_call(
        functools.partial(
            multiply_kernel,
            depth=slab_rows,
            span=span,
            first=first,
            count=count,
            added=len(extra),
        ),
        grid_spec=pltpu.PrefetchScalarGridSpec(
            num_scalar_prefetch=2,
            grid=(len(kinds), chips),
            in_specs=[pl.BlockSpec((slab_rows, count * slab_rows), rows_at)]
            + [pl.BlockSpec(piece.shape, lambda *at: (0, 0)) for piece in pieces]
            + [pl.BlockSpec(part, lambda h, i, *at: (h + base, i, 0, 0)) for _ in extra],
            out_specs=pl.BlockSpec(part, lambda h, i, *at: (h, i, 0, 0)),
            scratch_shapes=[pltpu.VMEM((count * slab_rows, width), BF16)],
        ),
        out_shape=jax.ShapeDtypeStruct((len(kinds), chips, slab_rows, width), F32),
        compiler_params=pltpu.CompilerParams(vmem_limit_bytes=21 * 1024 * 1024),
        cost_estimate=LITTLE,
    )(where, keeps, ancestor, *pieces, *extra)


def sum_kernel(where, mine_ref, handed_ref, own_ref, sent_ref):
    step = pl.program_id(0)
    summed = mine_ref[0, 0] + handed_ref[0, 0]
    depth, width = summed.shape

    @pl.when(step == 0)
    def _():
        own_ref[:depth, :] = summed
        own_ref[depth:, :] = jnp.zeros((TAIL, width), F32)

    @pl.when(step > 0)
    def _():
        most = jnp.max(jnp.abs(summed), axis=(0, 1), keepdims=True)
        power = jnp.ceil(jnp.log2(jnp.maximum(most, FLOOR)))
        sent_ref[0, :depth, :] = summed * jnp.exp2(TOP_POWER - power)
        sent_ref[0, depth:, :] = jnp.broadcast_to(power, (TAIL, width))


def chip_sum(where, mine, handed):
    chips, depth, width = mine.shape[1:]
    taken = pl.BlockSpec((1, 1, depth, width), lambda i, where: (0, where[2] ^ i, 0, 0))
    longer = depth + TAIL
    return pl.pallas_call(
        sum_kernel,
        grid_spec=pltpu.PrefetchScalarGridSpec(
            num_scalar_prefetch=1,
            grid=(chips,),
            in_specs=[taken, taken],
            out_specs=[
                pl.BlockSpec((longer, width), lambda *at: (0, 0)),
                pl.BlockSpec((1, longer, width), lambda i, *at: (jnp.maximum(i - 1, 0), 0, 0)),
            ],
        ),
        out_shape=[
            jax.ShapeDtypeStruct((longer, width), F32),
            jax.ShapeDtypeStruct((chips - 1, longer, width), F32),
        ],
        compiler_params=pltpu.CompilerParams(vmem_limit_bytes=15 * 1024 * 1024),
        cost_estimate=LITTLE,
    )(where, mine, handed)


def sibling(value, cols):
    return lax.ppermute(value, "col", [(c, c ^ 1) for c in range(cols)])


def to_chip(value, step, cols):
    return lax.ppermute(value, "col", [(c, c ^ (2 * step)) for c in range(cols)])


def after(value, others):
    return lax.optimization_barrier((value, others))[0]


def take(pieces, index):
    return lax.dynamic_index_in_dim(pieces, index, 0, keepdims=False)


def chip_scatter(summed, cols):
    chip = lax.axis_index("col") // 2
    total = take(summed, chip)
    arrived = [to_chip(take(summed, chip ^ step), step, cols) for step in range(1, cols // 2)]
    for piece in arrived:
        total = total + piece
    return total


def hand_over(payloads, cols):
    return [to_chip(payload, step + 1, cols) for step, payload in enumerate(payloads)]


def collect(own, arrived):
    longer, width = own.shape
    groups = (longer // SUBLANES, SUBLANES, width)
    total = own.reshape(groups)
    for payload in arrived:
        unit = jnp.exp2(payload[longer - TAIL :].astype(F32)[:SUBLANES] - TOP_POWER)
        total = total + payload.astype(F32).reshape(groups) * unit[None]
    return total.reshape(longer, width)


def small_kernel(where, keeps, sums, rows, couple, ends, stay_ref, give_ref):
    start, inner = ((0,), (0,)), ((1,), (0,))
    c_zero, c_one, c_two = couple[0], couple[1], couple[2]
    width = c_zero.shape[0]
    depth = rows.shape[0]
    unit = min(depth, width)

    def end(index):
        return jnp.where(where[4] == 0, ends[index], jnp.zeros_like(ends[index]))

    def turned(left, right):
        return split_dot(right, left, start).T

    def block(j, i):
        total = jnp.zeros((width, width), F32)
        for part in range(0, depth, unit):
            here = slice(part, part + unit)
            factor = rows[here, i * width : (i + 1) * width]
            factor = kept(keeps, i, where[4] + part, width, factor)
            total += split_dot(sums[here, j * width : (j + 1) * width], factor, start)
        return total

    t_oneone, t_twoone, t_threeone = block(0, 0), block(0, 1), block(0, 2)
    t_twotwo, t_threetwo, t_threethree = block(1, 1), block(1, 2), block(2, 2)
    m_twoone, m_threeone = t_twoone.T, t_threeone.T
    diag_one = end(0) + t_oneone.T
    cross_two = t_twoone - split_dot(diag_one, c_zero, inner)
    diag_two = (
        end(1) + t_twotwo.T - split_dot(m_twoone, c_zero, inner) - turned(c_zero, cross_two)
    )
    second_three = t_threetwo.T - split_dot(m_threeone, c_zero, inner)
    cross_first = t_threeone - split_dot(diag_one, c_one, inner) - split_dot(cross_two, c_two, inner)
    cross_second = (
        second_three.T
        - split_dot(cross_two, c_one, start)
        - split_dot(diag_two, c_two, inner)
    )
    diag_three = (
        end(2)
        + t_threethree.T
        - split_dot(m_threeone, c_one, inner)
        - split_dot(second_three, c_two, inner)
        - turned(c_one, cross_first)
        - turned(c_two, cross_second)
    )
    part = stay_ref.shape[2]
    blocks = (diag_one, diag_two, diag_three, cross_two, cross_first, cross_second)
    for index, value in enumerate(blocks):
        value = value.T
        for place in range(width // part):
            strip = value[place * part : (place + 1) * part, :]

            @pl.when(where[1] == place % 2)
            def _():
                stay_ref[place // 2, index] = strip

            @pl.when(where[1] != place % 2)
            def _():
                give_ref[place // 2, index] = strip


def small_parts(where, keeps, sums, rows, couplings, ends, cols):
    width = couplings.shape[1]
    whole = pl.BlockSpec(memory_space=pltpu.VMEM)
    scalars = pl.BlockSpec(memory_space=pltpu.SMEM)
    return pl.pallas_call(
        small_kernel,
        in_specs=[scalars] * 2 + [whole] * 4,
        out_specs=[whole] * 2,
        out_shape=[jax.ShapeDtypeStruct((cols // 2, 6, width // cols, width), F32)] * 2,
        compiler_params=pltpu.CompilerParams(vmem_limit_bytes=16 * 1024 * 1024),
        cost_estimate=LITTLE,
    )(where, keeps, sums, rows, couplings, ends)


def tile_scatter(stay, give, rows, cols):
    row, chip = lax.axis_index("row"), lax.axis_index("col") // 2
    held = stay + sibling(give, cols)
    arrived = [to_chip(take(held, chip ^ step), step, cols) for step in range(1, cols // 2)]
    held = functools.reduce(jnp.add, arrived, take(held, chip))
    bit = rows // 2
    while bit:
        size = held.shape[2] // 2
        side = row // bit % 2
        mine = lax.dynamic_slice_in_dim(held, side * size, size, 2)
        theirs = lax.dynamic_slice_in_dim(held, (1 - side) * size, size, 2)
        pairs = [(r, r ^ bit) for r in range(rows)]
        held = mine + lax.ppermute(theirs, "row", pairs)
        bit //= 2
    return jnp.swapaxes(held, 1, 2)


def body(
    rows,
    cols,
    ancestor,
    panel_one,
    panel_two,
    panel_three,
    couplings,
    diag_terms,
    list_two,
    list_three,
):
    block_width = couplings.shape[1]
    slab_rows = panel_one.shape[0]
    row_id, col_id = lax.axis_index("row"), lax.axis_index("col")
    device = row_id * cols + col_id
    core, chip = col_id % 2, col_id // 2
    others = [chip, col_id * ancestor.shape[1], device * slab_rows]
    turned_row = row_id ^ swap_of(col_id // (cols // rows), rows)
    where = jnp.stack([turned_row, core] + others).astype(jnp.int32)
    keep_two = piece_keep(list_two, device * slab_rows, slab_rows, block_width)
    keep_three = piece_keep(list_three, device * slab_rows, slab_rows, block_width)
    blocks = jnp.arange(ancestor.shape[0] * rows // block_width, dtype=jnp.int32)
    listed_two = jnp.any(blocks[:, None] == list_two[None, :], axis=1)
    listed_three = jnp.any(blocks[:, None] == list_three[None, :], axis=1)
    keeps = jnp.stack([jnp.ones_like(listed_two), listed_two, listed_three]).astype(jnp.int32)

    own_rows = join([panel_one, panel_two, panel_three])
    early, late = spread(own_rows, rows, cols)
    sums = multiply(where, keeps, ancestor, early, block_width, (0, 1))
    theirs = multiply(where, keeps, ancestor, late, block_width, (0,), sums)
    handed = sibling(theirs, cols)
    turn = after(where, theirs)
    mine = multiply(turn, keeps, ancestor, late, block_width, (1,), sums)
    own, sent = chip_sum(where, mine, handed)
    payloads = [sent[step].astype(F16) for step in range(cols // 2 - 1)]
    total = collect(own, hand_over(payloads, cols))
    parts = small_parts(where, keeps, total, own_rows, couplings, diag_terms, cols)
    own_tile = tile_scatter(*parts, rows, cols)
    sum_one = total[:slab_rows, :block_width]
    sum_two = total[:slab_rows, block_width : 2 * block_width]
    sum_three = total[:slab_rows, 2 * block_width :]
    inverse_one = -sum_one
    coupled = couplings.astype(F32)
    inverse_two = -(sum_two - product(sum_one, coupled[0])) * keep_two
    known = product(sum_one, coupled[1]) - product(inverse_two, coupled[2])
    inverse_three = (known - sum_three) * keep_three
    return (inverse_one, inverse_two, inverse_three, own_tile)


def solution(mesh):
    in_specs = (
        P("row", "col"),
        P(("row", "col"), None),
        P(("row", "col"), None),
        P(("row", "col"), None),
        P(),
        P(),
        P(),
        P(),
    )
    out_specs = (
        P(("row", "col"), None),
        P(("row", "col"), None),
        P(("row", "col"), None),
        P(None, "row", "col"),
    )
    local = functools.partial(body, mesh.shape["row"], mesh.shape["col"])
    return jax.shard_map(local, mesh=mesh, in_specs=in_specs, out_specs=out_specs, check_vma=False)
```

```python
import functools

import jax
import jax.numpy as jnp
from jax import lax
from jax.experimental import pallas as pl
from jax.experimental.pallas import tpu as pltpu
from jax.sharding import PartitionSpec as P

F32 = jnp.float32
BF16 = jnp.bfloat16
F16 = jnp.float16
TOP_POWER = 15.0
FLOOR = 2.0**-110
SUBLANES = 8
TAIL = 16
LITTLE = pl.CostEstimate(flops=1, bytes_accessed=1, transcendentals=0)


def product(former, latter):
    return jnp.dot(
        former, latter, precision=lax.Precision.HIGHEST, preferred_element_type=F32
    )


def piece_keep(listed, start_row, slab_rows, block_width):
    rows_here = start_row + jnp.arange(slab_rows, dtype=jnp.int32)
    matches = (rows_here // block_width)[:, None] == listed[None, :]
    return jnp.any(matches, axis=1).astype(F32)[:, None]


def swap_of(plane, rows):
    return plane % 2 * (rows // 2)


def spread_step(own, step, rows, cols):
    ratio = cols // rows
    pairs = []
    for plane in range(rows):
        for place in range(cols):
            to_plane = (place % rows) ^ step ^ swap_of(plane, rows)
            pairs.append((plane * cols + place, to_plane * cols + plane * ratio + place // rows))
    return lax.ppermute(own, ("row", "col"), pairs)


def spread(own, rows, cols):
    half = rows // 2
    early = [spread_step(own, step, rows, cols) for step in range(half)]
    late = [spread_step(after(own, early), half + step, rows, cols) for step in range(half)]
    return (0, early), (half, late)


def split_dot(former, latter, dims):
    high = former.astype(BF16)
    low = (former - high.astype(F32)).astype(BF16)
    dims = (dims, ((), ()))
    return lax.dot_general(high, latter, dims, preferred_element_type=F32) + lax.dot_general(
        low, latter, dims, preferred_element_type=F32
    )


def join_kernel(*refs):
    span = refs[0].shape[1]
    for index, panel_ref in enumerate(refs[:-1]):
        refs[-1][:, index * span : (index + 1) * span] = panel_ref[...]


def join(panels):
    rows, span = panels[0].shape
    whole = pl.BlockSpec(memory_space=pltpu.VMEM)
    return pl.pallas_call(
        join_kernel,
        in_specs=[whole] * len(panels),
        out_specs=whole,
        out_shape=jax.ShapeDtypeStruct((rows, span * len(panels)), panels[0].dtype),
        cost_estimate=LITTLE,
    )(*panels)


def kept(keeps, panel, row, span, value):
    return jnp.where(keeps[panel, row // span] > 0, value, jnp.zeros_like(value))


def multiply_kernel(where, keeps, s_ref, *refs, depth, span, first, count, added):
    out_ref, panel = refs[-2:]

    @pl.when((pl.program_id(0) == 0) & (pl.program_id(1) == 0))
    def _():
        unit = min(depth, span)
        for step in range(count):
            place = where[0] ^ (first + step)
            for part in range(0, depth, unit):
                target = pl.ds(pl.multiple_of(place % count * depth + part, unit), unit)
                row = where[3] + place * depth + part
                for index in range(panel.shape[1] // span):
                    lanes = slice(index * span, (index + 1) * span)
                    value = refs[step][part : part + unit, lanes]
                    panel[target, lanes] = kept(keeps, index, row, span, value)

    result = split_dot(s_ref[...], panel[...], ((1,), (0,)))
    if added:
        result += refs[count][0, 0]
    out_ref[0, 0] = result


def multiply(where, keeps, ancestor, run, span, kinds, added=None):
    first, pieces = run
    count = len(pieces)
    slab_rows, width = pieces[0].shape
    chips = ancestor.shape[0] // slab_rows // 2
    base = kinds[0]

    def rows_at(h, i, where, keeps):
        kind = jnp.where(h + base == 1, where[1], 1 - where[1])
        return 2 * i + kind, (where[0] ^ first) // count

    extra = [] if added is None else [added]
    part = (1, 1, slab_rows, width)
    return pl.pallas_call(
        functools.partial(
            multiply_kernel,
            depth=slab_rows,
            span=span,
            first=first,
            count=count,
            added=len(extra),
        ),
        grid_spec=pltpu.PrefetchScalarGridSpec(
            num_scalar_prefetch=2,
            grid=(len(kinds), chips),
            in_specs=[pl.BlockSpec((slab_rows, count * slab_rows), rows_at)]
            + [pl.BlockSpec(piece.shape, lambda *at: (0, 0)) for piece in pieces]
            + [pl.BlockSpec(part, lambda h, i, *at: (h + base, i, 0, 0)) for _ in extra],
            out_specs=pl.BlockSpec(part, lambda h, i, *at: (h, i, 0, 0)),
            scratch_shapes=[pltpu.VMEM((count * slab_rows, width), BF16)],
        ),
        out_shape=jax.ShapeDtypeStruct((len(kinds), chips, slab_rows, width), F32),
        compiler_params=pltpu.CompilerParams(vmem_limit_bytes=21 * 1024 * 1024),
        cost_estimate=LITTLE,
    )(where, keeps, ancestor, *pieces, *extra)


def sum_kernel(where, mine_ref, handed_ref, own_ref, sent_ref):
    step = pl.program_id(0)
    summed = mine_ref[0, 0] + handed_ref[0, 0]
    depth, width = summed.shape

    @pl.when(step == 0)
    def _():
        own_ref[:depth, :] = summed
        own_ref[depth:, :] = jnp.zeros((TAIL, width), F32)

    @pl.when(step > 0)
    def _():
        most = jnp.max(jnp.abs(summed), axis=(0, 1), keepdims=True)
        power = jnp.ceil(jnp.log2(jnp.maximum(most, FLOOR)))
        sent_ref[0, :depth, :] = summed * jnp.exp2(TOP_POWER - power)
        sent_ref[0, depth:, :] = jnp.broadcast_to(power, (TAIL, width))


def chip_sum(where, mine, handed):
    chips, depth, width = mine.shape[1:]
    taken = pl.BlockSpec((1, 1, depth, width), lambda i, where: (0, where[2] ^ i, 0, 0))
    longer = depth + TAIL
    return pl.pallas_call(
        sum_kernel,
        grid_spec=pltpu.PrefetchScalarGridSpec(
            num_scalar_prefetch=1,
            grid=(chips,),
            in_specs=[taken, taken],
            out_specs=[
                pl.BlockSpec((longer, width), lambda *at: (0, 0)),
                pl.BlockSpec((1, longer, width), lambda i, *at: (jnp.maximum(i - 1, 0), 0, 0)),
            ],
        ),
        out_shape=[
            jax.ShapeDtypeStruct((longer, width), F32),
            jax.ShapeDtypeStruct((chips - 1, longer, width), F32),
        ],
        compiler_params=pltpu.CompilerParams(vmem_limit_bytes=15 * 1024 * 1024),
        cost_estimate=LITTLE,
    )(where, mine, handed)


def sibling(value, cols):
    return lax.ppermute(value, "col", [(c, c ^ 1) for c in range(cols)])


def to_chip(value, step, cols):
    return lax.ppermute(value, "col", [(c, c ^ (2 * step)) for c in range(cols)])


def after(value, others):
    return lax.optimization_barrier((value, others))[0]


def take(pieces, index):
    return lax.dynamic_index_in_dim(pieces, index, 0, keepdims=False)


def chip_scatter(summed, cols):
    chip = lax.axis_index("col") // 2
    total = take(summed, chip)
    arrived = [to_chip(take(summed, chip ^ step), step, cols) for step in range(1, cols // 2)]
    for piece in arrived:
        total = total + piece
    return total


def hand_over(payloads, cols):
    return [to_chip(payload, step + 1, cols) for step, payload in enumerate(payloads)]


def collect(own, arrived):
    longer, width = own.shape
    groups = (longer // SUBLANES, SUBLANES, width)
    total = own.reshape(groups)
    for payload in arrived:
        unit = jnp.exp2(payload[longer - TAIL :].astype(F32)[:SUBLANES] - TOP_POWER)
        total = total + payload.astype(F32).reshape(groups) * unit[None]
    return total.reshape(longer, width)


def small_kernel(where, keeps, sums, rows, couple, ends, stay_ref, give_ref):
    start, inner = ((0,), (0,)), ((1,), (0,))
    c_zero, c_one, c_two = couple[0], couple[1], couple[2]
    width = c_zero.shape[0]
    depth = rows.shape[0]
    unit = min(depth, width)

    def end(index):
        return jnp.where(where[4] == 0, ends[index], jnp.zeros_like(ends[index]))

    def turned(left, right):
        return split_dot(right, left, start).T

    def block(j, i):
        total = jnp.zeros((width, width), F32)
        for part in range(0, depth, unit):
            here = slice(part, part + unit)
            factor = rows[here, i * width : (i + 1) * width]
            factor = kept(keeps, i, where[4] + part, width, factor)
            total += split_dot(sums[here, j * width : (j + 1) * width], factor, start)
        return total

    t_oneone, t_twoone, t_threeone = block(0, 0), block(0, 1), block(0, 2)
    t_twotwo, t_threetwo, t_threethree = block(1, 1), block(1, 2), block(2, 2)
    m_twoone, m_threeone = t_twoone.T, t_threeone.T
    diag_one = end(0) + t_oneone.T
    cross_two = t_twoone - split_dot(diag_one, c_zero, inner)
    diag_two = (
        end(1) + t_twotwo.T - split_dot(m_twoone, c_zero, inner) - turned(c_zero, cross_two)
    )
    second_three = t_threetwo.T - split_dot(m_threeone, c_zero, inner)
    cross_first = t_threeone - split_dot(diag_one, c_one, inner) - split_dot(cross_two, c_two, inner)
    cross_second = (
        second_three.T
        - split_dot(cross_two, c_one, start)
        - split_dot(diag_two, c_two, inner)
    )
    diag_three = (
        end(2)
        + t_threethree.T
        - split_dot(m_threeone, c_one, inner)
        - split_dot(second_three, c_two, inner)
        - turned(c_one, cross_first)
        - turned(c_two, cross_second)
    )
    part = stay_ref.shape[2]
    blocks = (diag_one, diag_two, diag_three, cross_two, cross_first, cross_second)
    for index, value in enumerate(blocks):
        value = value.T
        for place in range(width // part):
            strip = value[place * part : (place + 1) * part, :]

            @pl.when(where[1] == place % 2)
            def _():
                stay_ref[place // 2, index] = strip

            @pl.when(where[1] != place % 2)
            def _():
                give_ref[place // 2, index] = strip


def small_parts(where, keeps, sums, rows, couplings, ends, cols):
    width = couplings.shape[1]
    whole = pl.BlockSpec(memory_space=pltpu.VMEM)
    scalars = pl.BlockSpec(memory_space=pltpu.SMEM)
    return pl.pallas_call(
        small_kernel,
        in_specs=[scalars] * 2 + [whole] * 4,
        out_specs=[whole] * 2,
        out_shape=[jax.ShapeDtypeStruct((cols // 2, 6, width // cols, width), F32)] * 2,
        compiler_params=pltpu.CompilerParams(vmem_limit_bytes=16 * 1024 * 1024),
        cost_estimate=LITTLE,
    )(where, keeps, sums, rows, couplings, ends)


def tile_scatter(stay, give, rows, cols):
    row, chip = lax.axis_index("row"), lax.axis_index("col") // 2
    held = stay + sibling(give, cols)
    arrived = [to_chip(take(held, chip ^ step), step, cols) for step in range(1, cols // 2)]
    held = functools.reduce(jnp.add, arrived, take(held, chip))
    size = held.shape[2] // rows

    def rows_of(plane):
        return lax.dynamic_slice_in_dim(held, plane * size, size, 2)

    total = rows_of(row)
    for step in range(1, rows):
        pairs = [(r, r ^ step) for r in range(rows)]
        total = total + lax.ppermute(rows_of(row ^ step), "row", pairs)
    return jnp.swapaxes(total, 1, 2)


def body(
    rows,
    cols,
    ancestor,
    panel_one,
    panel_two,
    panel_three,
    couplings,
    diag_terms,
    list_two,
    list_three,
):
    block_width = couplings.shape[1]
    slab_rows = panel_one.shape[0]
    row_id, col_id = lax.axis_index("row"), lax.axis_index("col")
    device = row_id * cols + col_id
    core, chip = col_id % 2, col_id // 2
    others = [chip, col_id * ancestor.shape[1], device * slab_rows]
    turned_row = row_id ^ swap_of(col_id // (cols // rows), rows)
    where = jnp.stack([turned_row, core] + others).astype(jnp.int32)
    keep_two = piece_keep(list_two, device * slab_rows, slab_rows, block_width)
    keep_three = piece_keep(list_three, device * slab_rows, slab_rows, block_width)
    blocks = jnp.arange(ancestor.shape[0] * rows // block_width, dtype=jnp.int32)
    listed_two = jnp.any(blocks[:, None] == list_two[None, :], axis=1)
    listed_three = jnp.any(blocks[:, None] == list_three[None, :], axis=1)
    keeps = jnp.stack([jnp.ones_like(listed_two), listed_two, listed_three]).astype(jnp.int32)

    own_rows = join([panel_one, panel_two, panel_three])
    early, late = spread(own_rows, rows, cols)
    sums = multiply(where, keeps, ancestor, early, block_width, (0, 1))
    theirs = multiply(where, keeps, ancestor, late, block_width, (0,), sums)
    handed = sibling(theirs, cols)
    turn = after(where, theirs)
    mine = multiply(turn, keeps, ancestor, late, block_width, (1,), sums)
    own, sent = chip_sum(where, mine, handed)
    payloads = [sent[step].astype(F16) for step in range(cols // 2 - 1)]
    total = collect(own, hand_over(payloads, cols))
    parts = small_parts(where, keeps, total, own_rows, couplings, diag_terms, cols)
    own_tile = tile_scatter(*parts, rows, cols)
    sum_one = total[:slab_rows, :block_width]
    sum_two = total[:slab_rows, block_width : 2 * block_width]
    sum_three = total[:slab_rows, 2 * block_width :]
    inverse_one = -sum_one
    coupled = couplings.astype(F32)
    inverse_two = -(sum_two - product(sum_one, coupled[0])) * keep_two
    known = product(sum_one, coupled[1]) - product(inverse_two, coupled[2])
    inverse_three = (known - sum_three) * keep_three
    return (inverse_one, inverse_two, inverse_three, own_tile)


def solution(mesh):
    in_specs = (
        P("row", "col"),
        P(("row", "col"), None),
        P(("row", "col"), None),
        P(("row", "col"), None),
        P(),
        P(),
        P(),
        P(),
    )
    out_specs = (
        P(("row", "col"), None),
        P(("row", "col"), None),
        P(("row", "col"), None),
        P(None, "row", "col"),
    )
    local = functools.partial(body, mesh.shape["row"], mesh.shape["col"])
    return jax.shard_map(local, mesh=mesh, in_specs=in_specs, out_specs=out_specs, check_vma=False)
```

```python
import functools

import jax
import jax.numpy as jnp
from jax import lax
from jax.experimental import pallas as pl
from jax.experimental.pallas import tpu as pltpu
from jax.sharding import PartitionSpec as P

F32 = jnp.float32
BF16 = jnp.bfloat16
F16 = jnp.float16
TOP_POWER = 15.0
FLOOR = 2.0**-110
SUBLANES = 8
TAIL = 16
LITTLE = pl.CostEstimate(flops=1, bytes_accessed=1, transcendentals=0)


def product(former, latter):
    return jnp.dot(
        former, latter, precision=lax.Precision.HIGHEST, preferred_element_type=F32
    )


def piece_keep(listed, start_row, slab_rows, block_width):
    rows_here = start_row + jnp.arange(slab_rows, dtype=jnp.int32)
    matches = (rows_here // block_width)[:, None] == listed[None, :]
    return jnp.any(matches, axis=1).astype(F32)[:, None]


def swap_of(plane, rows):
    return plane % 2 * (rows // 2)


def spread_step(own, step, rows, cols):
    ratio = cols // rows
    pairs = []
    for plane in range(rows):
        for place in range(cols):
            to_plane = (place % rows) ^ step ^ swap_of(plane, rows)
            pairs.append((plane * cols + place, to_plane * cols + plane * ratio + place // rows))
    return lax.ppermute(own, ("row", "col"), pairs)


def spread(own, rows, cols):
    half = rows // 2
    early = [spread_step(own, step, rows, cols) for step in range(half)]
    late = [spread_step(after(own, early), half + step, rows, cols) for step in range(half)]
    return (0, early), (half, late)


def split_dot(former, latter, dims):
    high = former.astype(BF16)
    low = (former - high.astype(F32)).astype(BF16)
    dims = (dims, ((), ()))
    return lax.dot_general(high, latter, dims, preferred_element_type=F32) + lax.dot_general(
        low, latter, dims, preferred_element_type=F32
    )


def join_kernel(*refs):
    span = refs[0].shape[1]
    for index, panel_ref in enumerate(refs[:-1]):
        refs[-1][:, index * span : (index + 1) * span] = panel_ref[...]


def join(panels):
    rows, span = panels[0].shape
    whole = pl.BlockSpec(memory_space=pltpu.VMEM)
    return pl.pallas_call(
        join_kernel,
        in_specs=[whole] * len(panels),
        out_specs=whole,
        out_shape=jax.ShapeDtypeStruct((rows, span * len(panels)), panels[0].dtype),
        cost_estimate=LITTLE,
    )(*panels)


def kept(keeps, panel, row, span, value):
    return jnp.where(keeps[panel, row // span] > 0, value, jnp.zeros_like(value))


def multiply_kernel(where, keeps, s_ref, *refs, depth, span, first, count, added):
    out_ref, panel = refs[-2:]

    @pl.when((pl.program_id(0) == 0) & (pl.program_id(1) == 0))
    def _():
        unit = min(depth, span)
        for step in range(count):
            place = where[0] ^ (first + step)
            for part in range(0, depth, unit):
                target = pl.ds(pl.multiple_of(place % count * depth + part, unit), unit)
                row = where[3] + place * depth + part
                for index in range(panel.shape[1] // span):
                    lanes = slice(index * span, (index + 1) * span)
                    value = refs[step][part : part + unit, lanes]
                    panel[target, lanes] = kept(keeps, index, row, span, value)

    result = split_dot(s_ref[...], panel[...], ((1,), (0,)))
    if added:
        result += refs[count][0, 0]
    out_ref[0, 0] = result


def multiply(where, keeps, ancestor, run, span, kinds, added=None):
    first, pieces = run
    count = len(pieces)
    slab_rows, width = pieces[0].shape
    chips = ancestor.shape[0] // slab_rows // 2
    base = kinds[0]

    def rows_at(h, i, where, keeps):
        kind = jnp.where(h + base == 1, where[1], 1 - where[1])
        return 2 * i + kind, (where[0] ^ first) // count

    extra = [] if added is None else [added]
    part = (1, 1, slab_rows, width)
    return pl.pallas_call(
        functools.partial(
            multiply_kernel,
            depth=slab_rows,
            span=span,
            first=first,
            count=count,
            added=len(extra),
        ),
        grid_spec=pltpu.PrefetchScalarGridSpec(
            num_scalar_prefetch=2,
            grid=(len(kinds), chips),
            in_specs=[pl.BlockSpec((slab_rows, count * slab_rows), rows_at)]
            + [pl.BlockSpec(piece.shape, lambda *at: (0, 0)) for piece in pieces]
            + [pl.BlockSpec(part, lambda h, i, *at: (h + base, i, 0, 0)) for _ in extra],
            out_specs=pl.BlockSpec(part, lambda h, i, *at: (h, i, 0, 0)),
            scratch_shapes=[pltpu.VMEM((count * slab_rows, width), BF16)],
        ),
        out_shape=jax.ShapeDtypeStruct((len(kinds), chips, slab_rows, width), F32),
        compiler_params=pltpu.CompilerParams(vmem_limit_bytes=21 * 1024 * 1024),
        cost_estimate=LITTLE,
    )(where, keeps, ancestor, *pieces, *extra)


def sum_kernel(where, mine_ref, handed_ref, own_ref, sent_ref):
    step = pl.program_id(0)
    summed = mine_ref[0, 0] + handed_ref[0, 0]
    depth, width = summed.shape

    @pl.when(step == 0)
    def _():
        own_ref[:depth, :] = summed
        own_ref[depth:, :] = jnp.zeros((TAIL, width), F32)

    @pl.when(step > 0)
    def _():
        most = jnp.max(jnp.abs(summed), axis=(0, 1), keepdims=True)
        power = jnp.ceil(jnp.log2(jnp.maximum(most, FLOOR)))
        sent_ref[0, :depth, :] = summed * jnp.exp2(TOP_POWER - power)
        sent_ref[0, depth:, :] = jnp.broadcast_to(power, (TAIL, width))


def chip_sum(where, mine, handed):
    chips, depth, width = mine.shape[1:]
    taken = pl.BlockSpec((1, 1, depth, width), lambda i, where: (0, where[2] ^ i, 0, 0))
    longer = depth + TAIL
    return pl.pallas_call(
        sum_kernel,
        grid_spec=pltpu.PrefetchScalarGridSpec(
            num_scalar_prefetch=1,
            grid=(chips,),
            in_specs=[taken, taken],
            out_specs=[
                pl.BlockSpec((longer, width), lambda *at: (0, 0)),
                pl.BlockSpec((1, longer, width), lambda i, *at: (jnp.maximum(i - 1, 0), 0, 0)),
            ],
        ),
        out_shape=[
            jax.ShapeDtypeStruct((longer, width), F32),
            jax.ShapeDtypeStruct((chips - 1, longer, width), F32),
        ],
        compiler_params=pltpu.CompilerParams(vmem_limit_bytes=15 * 1024 * 1024),
        cost_estimate=LITTLE,
    )(where, mine, handed)


def sibling(value, cols):
    return lax.ppermute(value, "col", [(c, c ^ 1) for c in range(cols)])


def to_chip(value, step, cols):
    return lax.ppermute(value, "col", [(c, c ^ (2 * step)) for c in range(cols)])


def after(value, others):
    return lax.optimization_barrier((value, others))[0]


def take(pieces, index):
    return lax.dynamic_index_in_dim(pieces, index, 0, keepdims=False)


def chip_scatter(summed, cols):
    chip = lax.axis_index("col") // 2
    total = take(summed, chip)
    arrived = [to_chip(take(summed, chip ^ step), step, cols) for step in range(1, cols // 2)]
    for piece in arrived:
        total = total + piece
    return total


def hand_over(payloads, cols):
    return [to_chip(payload, step + 1, cols) for step, payload in enumerate(payloads)]


def collect(own, arrived):
    longer, width = own.shape
    groups = (longer // SUBLANES, SUBLANES, width)
    total = own.reshape(groups)
    for payload in arrived:
        unit = jnp.exp2(payload[longer - TAIL :].astype(F32)[:SUBLANES] - TOP_POWER)
        total = total + payload.astype(F32).reshape(groups) * unit[None]
    return total.reshape(longer, width)


def small_kernel(where, keeps, sums, rows, couple, ends, stay_ref, give_ref):
    start, inner = ((0,), (0,)), ((1,), (0,))
    c_zero, c_one, c_two = couple[0], couple[1], couple[2]
    width = c_zero.shape[0]
    depth = rows.shape[0]
    unit = min(depth, width)

    def end(index):
        return jnp.where(where[4] == 0, ends[index], jnp.zeros_like(ends[index]))

    def turned(left, right):
        return split_dot(right, left, start).T

    def block(j, i):
        total = jnp.zeros((width, width), F32)
        for part in range(0, depth, unit):
            here = slice(part, part + unit)
            factor = rows[here, i * width : (i + 1) * width]
            factor = kept(keeps, i, where[4] + part, width, factor)
            total += split_dot(sums[here, j * width : (j + 1) * width], factor, start)
        return total

    t_oneone, t_twoone, t_threeone = block(0, 0), block(0, 1), block(0, 2)
    t_twotwo, t_threetwo, t_threethree = block(1, 1), block(1, 2), block(2, 2)
    m_twoone, m_threeone = t_twoone.T, t_threeone.T
    diag_one = end(0) + t_oneone.T
    cross_two = t_twoone - split_dot(diag_one, c_zero, inner)
    diag_two = (
        end(1) + t_twotwo.T - split_dot(m_twoone, c_zero, inner) - turned(c_zero, cross_two)
    )
    second_three = t_threetwo.T - split_dot(m_threeone, c_zero, inner)
    cross_first = t_threeone - split_dot(diag_one, c_one, inner) - split_dot(cross_two, c_two, inner)
    cross_second = (
        second_three.T
        - split_dot(cross_two, c_one, start)
        - split_dot(diag_two, c_two, inner)
    )
    diag_three = (
        end(2)
        + t_threethree.T
        - split_dot(m_threeone, c_one, inner)
        - split_dot(second_three, c_two, inner)
        - turned(c_one, cross_first)
        - turned(c_two, cross_second)
    )
    part = stay_ref.shape[2]
    blocks = (diag_one, diag_two, diag_three, cross_two, cross_first, cross_second)
    for index, value in enumerate(blocks):
        value = value.T
        for place in range(width // part):
            strip = value[place * part : (place + 1) * part, :]

            @pl.when(where[1] == place % 2)
            def _():
                stay_ref[place // 2, index] = strip

            @pl.when(where[1] != place % 2)
            def _():
                give_ref[place // 2, index] = strip


def small_parts(where, keeps, sums, rows, couplings, ends, cols):
    width = couplings.shape[1]
    whole = pl.BlockSpec(memory_space=pltpu.VMEM)
    scalars = pl.BlockSpec(memory_space=pltpu.SMEM)
    return pl.pallas_call(
        small_kernel,
        in_specs=[scalars] * 2 + [whole] * 4,
        out_specs=[whole] * 2,
        out_shape=[jax.ShapeDtypeStruct((cols // 2, 6, width // cols, width), F32)] * 2,
        compiler_params=pltpu.CompilerParams(vmem_limit_bytes=16 * 1024 * 1024),
        cost_estimate=LITTLE,
    )(where, keeps, sums, rows, couplings, ends)


def tile_scatter(stay, give, rows, cols):
    row, chip = lax.axis_index("row"), lax.axis_index("col") // 2
    handed = sibling(give, cols)
    sums = [take(stay, chip ^ step) + take(handed, chip ^ step) for step in range(cols // 2)]
    arrived = [to_chip(part, step, cols) for step, part in enumerate(sums) if step]
    held = functools.reduce(jnp.add, arrived, sums[0])
    bit = rows // 2
    while bit:
        size = held.shape[2] // 2
        side = row // bit % 2
        mine = lax.dynamic_slice_in_dim(held, side * size, size, 2)
        theirs = lax.dynamic_slice_in_dim(held, (1 - side) * size, size, 2)
        pairs = [(r, r ^ bit) for r in range(rows)]
        held = mine + lax.ppermute(theirs, "row", pairs)
        bit //= 2
    return jnp.swapaxes(held, 1, 2)


def body(
    rows,
    cols,
    ancestor,
    panel_one,
    panel_two,
    panel_three,
    couplings,
    diag_terms,
    list_two,
    list_three,
):
    block_width = couplings.shape[1]
    slab_rows = panel_one.shape[0]
    row_id, col_id = lax.axis_index("row"), lax.axis_index("col")
    device = row_id * cols + col_id
    core, chip = col_id % 2, col_id // 2
    others = [chip, col_id * ancestor.shape[1], device * slab_rows]
    turned_row = row_id ^ swap_of(col_id // (cols // rows), rows)
    where = jnp.stack([turned_row, core] + others).astype(jnp.int32)
    keep_two = piece_keep(list_two, device * slab_rows, slab_rows, block_width)
    keep_three = piece_keep(list_three, device * slab_rows, slab_rows, block_width)
    blocks = jnp.arange(ancestor.shape[0] * rows // block_width, dtype=jnp.int32)
    listed_two = jnp.any(blocks[:, None] == list_two[None, :], axis=1)
    listed_three = jnp.any(blocks[:, None] == list_three[None, :], axis=1)
    keeps = jnp.stack([jnp.ones_like(listed_two), listed_two, listed_three]).astype(jnp.int32)

    own_rows = join([panel_one, panel_two, panel_three])
    early, late = spread(own_rows, rows, cols)
    sums = multiply(where, keeps, ancestor, early, block_width, (0, 1))
    theirs = multiply(where, keeps, ancestor, late, block_width, (0,), sums)
    handed = sibling(theirs, cols)
    turn = after(where, theirs)
    mine = multiply(turn, keeps, ancestor, late, block_width, (1,), sums)
    own, sent = chip_sum(where, mine, handed)
    payloads = [sent[step].astype(F16) for step in range(cols // 2 - 1)]
    total = collect(own, hand_over(payloads, cols))
    parts = small_parts(where, keeps, total, own_rows, couplings, diag_terms, cols)
    own_tile = tile_scatter(*parts, rows, cols)
    sum_one = total[:slab_rows, :block_width]
    sum_two = total[:slab_rows, block_width : 2 * block_width]
    sum_three = total[:slab_rows, 2 * block_width :]
    inverse_one = -sum_one
    coupled = couplings.astype(F32)
    inverse_two = -(sum_two - product(sum_one, coupled[0])) * keep_two
    known = product(sum_one, coupled[1]) - product(inverse_two, coupled[2])
    inverse_three = (known - sum_three) * keep_three
    return (inverse_one, inverse_two, inverse_three, own_tile)


def solution(mesh):
    in_specs = (
        P("row", "col"),
        P(("row", "col"), None),
        P(("row", "col"), None),
        P(("row", "col"), None),
        P(),
        P(),
        P(),
        P(),
    )
    out_specs = (
        P(("row", "col"), None),
        P(("row", "col"), None),
        P(("row", "col"), None),
        P(None, "row", "col"),
    )
    local = functools.partial(body, mesh.shape["row"], mesh.shape["col"])
    return jax.shard_map(local, mesh=mesh, in_specs=in_specs, out_specs=out_specs, check_vma=False)
```
